32 devices in a mesh: seq: 2 (over core), dp: 4 (over y, x), tensor: 4 (over z).
Axes of the slice: x: 2, y: 2, z: 4, core: 2. Of those that a mesh axis runs over, the one named last changes fastest.
Arguments:
- attention_queries: bfloat16 [4, 256, 3584], P('dp', 'seq', 'tensor')
- attention_keys: bfloat16 [4, 256, 512], P('dp', 'seq', 'tensor')
- attention_values: bfloat16 [4, 256, 512], P('dp', 'seq', 'tensor')
- key_window_length: int32 [4], P('tensor'), may hold values from 128 to 512, as said below
- norm_gain: float32 [3584], P('tensor'), may hold values from 0.5 to 2
- spike_levels: int32 [3584], P('tensor'), may hold values from 1 to 4
- lin_queries: bfloat16 [4, 256, 3584], P('dp', 'seq', 'tensor'), may hold values from -6 to 6
- lin_keys: bfloat16 [4, 256, 3584], P('dp', 'seq', 'tensor'), may hold values from -6 to 6
- decay_logs: float32 [4, 28, 256], P('dp', 'tensor', 'seq'), as said below
- cotangent: bfloat16 [4, 256, 3584], P('dp', 'seq', 'tensor')
Outputs:
- layer_output: bfloat16 [4, 256, 3584], P('dp', 'seq', 'tensor')
- query_grads: bfloat16 [4, 256, 3584], P('dp', 'seq', 'tensor')
- key_gradient: bfloat16 [4, 256, 512], P('dp', 'seq', 'tensor')
- value_gradient: bfloat16 [4, 256, 512], P('dp', 'seq', 'tensor')
- gain_grads: float32 [3584], P('tensor')
The draws below stay inside these ranges and needn't reach their ends.
Inputs may be any that keep to these rules, and one draw needn't show every extreme that they name: Key head g lets query t see positions j with t - key_window_length[g] < j <= t; some head has exactly 512. `decay_logs`: non-positive.
All inputs are finite; a program needn't handle non-finite values.
Results may differ from the reference program's by a relative error of at most 0.015.
Values may be sent and summed in bfloat16 or wider, within the bound.
A program may use at most 128 MiB of HBM per device.

```python
import math
import jax
import jax.numpy as jnp
from jax import lax

TEST_LANES = 28
KEY_VALUE_HEADS = 4
HEAD_SIZE = 128
D = 3584
LONGEST_WINDOW = 512
SEQUENCE_SHARD = 128
LENGTH = 256
BATCH = 4
N_SEQ = 2
N_DP = 4


def attention_draw(key):
    base_offset = jax.random.fold_in(key, 7)
    key_query, random_keys_split = jax.random.split(base_offset, 2)
    batch_count = N_DP
    whole_span = SEQUENCE_SHARD * N_SEQ
    query_block = jax.random.normal(key_query, (batch_count, whole_span, TEST_LANES, HEAD_SIZE), jnp.float32)
    key_row_block = jax.random.normal(random_keys_split, (batch_count, whole_span, KEY_VALUE_HEADS, HEAD_SIZE), jnp.float32)
    return (query_block, key_row_block)


def draw_attention_queries(key, part):
    query_block, key_row_block = attention_draw(key)
    return query_block.reshape(N_DP, SEQUENCE_SHARD * N_SEQ, TEST_LANES * HEAD_SIZE).astype(jnp.bfloat16)


def draw_attention_keys(key, part):
    query_block, key_row_block = attention_draw(key)
    return key_row_block.reshape(N_DP, SEQUENCE_SHARD * N_SEQ, KEY_VALUE_HEADS * HEAD_SIZE).astype(jnp.bfloat16)


def draw_attention_values(key, part):
    whole_span = SEQUENCE_SHARD * N_SEQ
    random_main_key = jax.random.fold_in(jax.random.fold_in(key, 3), 0)
    scale_factors = 3.0 ** (jnp.arange(KEY_VALUE_HEADS, dtype=jnp.float32) / max(KEY_VALUE_HEADS - 1, 1))
    base_offset = jax.random.normal(random_main_key, (N_DP, whole_span, KEY_VALUE_HEADS, HEAD_SIZE), jnp.float32)
    return (base_offset * scale_factors[:, None]).reshape(N_DP, whole_span, KEY_VALUE_HEADS * HEAD_SIZE).astype(jnp.bfloat16)


def draw_key_window_length(key, part):
    random_draw_key, random_pick_key = jax.random.split(jax.random.fold_in(key, 5))
    drawn_sample = jax.random.randint(random_draw_key, (KEY_VALUE_HEADS,), LONGEST_WINDOW // 4, LONGEST_WINDOW + 1)
    chosen_heads = jax.random.randint(random_pick_key, (), 0, KEY_VALUE_HEADS)
    return drawn_sample.at[chosen_heads].set(LONGEST_WINDOW)


def draw_decay_logs(key, part):
    whole_span = SEQUENCE_SHARD * N_SEQ
    divided_slices = jax.random.split(jax.random.fold_in(key, 9), 6)
    fast_odds = 2
    quick_pointer = jax.random.randint(divided_slices[0], (N_DP, TEST_LANES, 1), 0, fast_odds) == 0
    lookback_span = jax.random.uniform(divided_slices[1], (N_DP, TEST_LANES, 1), jnp.float32, 30.0, 50.0)
    gentle_pointer = jax.random.uniform(divided_slices[2], (N_DP, TEST_LANES, 1), jnp.float32, 0.1, 0.5) / whole_span
    coarse_estimate = jnp.exp(jax.random.uniform(divided_slices[3], (N_DP, TEST_LANES, whole_span), jnp.float32, -0.7, 0.7))
    pulse_ratios = jnp.where(quick_pointer, 1.0 / lookback_span, gentle_pointer) * coarse_estimate
    pulse_occasions = jax.random.randint(divided_slices[4], (N_DP, TEST_LANES, 2), 0, whole_span)
    thrown_items = jnp.log(jax.random.uniform(divided_slices[5], (N_DP, TEST_LANES, 2), jnp.float32, 0.5, 0.8))
    symbol_place = jnp.arange(N_DP)[:, None, None]
    lane_ordinal = jnp.arange(TEST_LANES)[None, :, None]
    return (-pulse_ratios).at[symbol_place, lane_ordinal, pulse_occasions].add(thrown_items)


def draw_cotangent(key, part):
    whole_span = SEQUENCE_SHARD * N_SEQ
    random_main_key = jax.random.fold_in(key, 13)
    position = jnp.arange(whole_span, dtype=jnp.float32) / max(whole_span - 1, 1)
    sequence = jnp.arange(N_DP, dtype=jnp.float32) / max(N_DP - 1, 1)
    scale_factors = (1.0 + 2.0 * position)[None, :, None] * (1.0 + sequence)[:, None, None]
    base_offset = jax.random.normal(random_main_key, (N_DP, whole_span, TEST_LANES * HEAD_SIZE), jnp.float32)
    return (base_offset * scale_factors).astype(jnp.bfloat16)


def with_ends(array, stream_key, least, high):
    index_at = [jax.random.randint(jax.random.fold_in(stream_key, axis), (), 0, length) for axis, length in enumerate(array.shape)]
    longest = array.shape.index(max(array.shape))
    next_to = index_at[:longest] + [(index_at[longest] + 1) % array.shape[longest]] + index_at[longest + 1:]
    return array.at[tuple(index_at)].set(least).at[tuple(next_to)].set(high)


def shard_levels(stream_key, dims, pieces, smallest, largest):
    def one(axis_at, blocks):
        steps = jax.random.uniform(jax.random.fold_in(jax.random.fold_in(stream_key, 6), axis_at), (blocks,), jnp.float32, smallest / len(pieces), largest / len(pieces))
        return jnp.repeat(jnp.exp(steps), dims[axis_at] // blocks).reshape((-1,) + (1,) * (len(dims) - axis_at - 1))

    gain = one(*pieces[0])
    for cut in pieces[1:]:
        gain = gain * one(*cut)
    return gain


def gaussian(rng, shape, deviation, reach, pieces=(), held_as=jnp.bfloat16):
    drawn = deviation * jax.random.normal(rng, shape, jnp.float32)
    if pieces:
        drawn = drawn * shard_levels(rng, shape, pieces, -0.22, 0.18)
    return jnp.clip(drawn, -reach, reach).astype(held_as)


def setup_inputs(seed: int = 0) -> dict:
    splits = jax.random.split(jax.random.key(seed), 11)
    return {
        "attention_queries": draw_attention_queries(jax.random.fold_in(splits[10], 71), 0),
        "attention_keys": draw_attention_keys(jax.random.fold_in(splits[10], 71), 0),
        "attention_values": draw_attention_values(jax.random.fold_in(splits[10], 71), 0),
        "key_window_length": draw_key_window_length(jax.random.fold_in(splits[10], 71), 0),
        "norm_gain": jnp.clip(jnp.exp(math.log(2.0) - 1.3862944 * jax.random.uniform(splits[4], (D,), jnp.float32) ** shard_levels(splits[4], (D,), ((0, 4),), -0.2, 0.2)), 0.5, 2.0),
        "spike_levels": with_ends(jax.random.randint(splits[5], (D,), 1, 5), jax.random.fold_in(splits[5], 1), 1, 4).astype(jnp.int32),
        "lin_queries": gaussian(splits[6], (BATCH, LENGTH, D), 1.0, 6.0, ((0, 4), (1, 2), (2, 4))),
        "lin_keys": gaussian(splits[7], (BATCH, LENGTH, D), 1.0, 6.0, ((0, 4), (1, 2), (2, 4))),
        "decay_logs": draw_decay_logs(jax.random.fold_in(splits[10], 71), 0),
        "cotangent": draw_cotangent(jax.random.fold_in(splits[10], 71), 0),
    }


precise = lax.Precision.HIGHEST
epsilon = 1e-06

def masked_logits(query_block, key_row_block, first_query, key_reach):
    block_rows = query_block.shape[1]
    key_span = key_row_block.shape[0] - block_rows
    scaling = 1.0 / math.sqrt(query_block.shape[2])
    logits = jnp.einsum('gsd,kd->gsk', query_block.astype(jnp.float32), key_row_block.astype(jnp.float32)) * scaling
    query_pos = first_query + jnp.arange(block_rows, dtype=jnp.int32)[:, None]
    key_pos = first_query - key_span + jnp.arange(key_row_block.shape[0], dtype=jnp.int32)[None, :]
    allowed = (key_pos >= 0) & (key_pos <= query_pos) & (key_pos > query_pos - key_reach)
    return (jnp.where(allowed[None], logits, -jnp.inf), scaling)

def padded_window(group_keys):
    key_span = (LONGEST_WINDOW + SEQUENCE_SHARD - 1) // SEQUENCE_SHARD * SEQUENCE_SHARD
    padding = jnp.zeros((key_span, group_keys.shape[1]), group_keys.dtype)
    return (jnp.concatenate([padding, group_keys], axis=0), key_span)

def attend_forward(group_queries, group_keys, group_values, key_reach):
    whole_span = group_keys.shape[0]
    padded_keys, key_span = padded_window(group_keys)
    padded_values, key_span = padded_window(group_values)

    def one_block(block_index):
        first_query = block_index * SEQUENCE_SHARD
        query_block = lax.dynamic_slice_in_dim(group_queries, first_query, SEQUENCE_SHARD, 1)
        key_row_block = lax.dynamic_slice_in_dim(padded_keys, first_query, key_span + SEQUENCE_SHARD, 0)
        value_rows = lax.dynamic_slice_in_dim(padded_values, first_query, key_span + SEQUENCE_SHARD, 0)
        logits, scaling = masked_logits(query_block, key_row_block, first_query, key_reach)
        row_max = lax.optimization_barrier(jnp.max(logits, axis=-1))
        exponent = jnp.exp(logits - row_max[..., None])
        row_sum = lax.optimization_barrier(jnp.sum(exponent, axis=-1))
        weights = (exponent / row_sum[..., None]).astype(jnp.bfloat16)
        output = jnp.einsum('gsk,kd->gsd', weights.astype(jnp.float32), value_rows.astype(jnp.float32))
        return (output.astype(jnp.bfloat16), row_max, row_sum)
    outputs, maxima, sums = lax.map(one_block, jnp.arange(whole_span // SEQUENCE_SHARD, dtype=jnp.int32))
    head_groups = group_queries.shape[0]
    outputs = outputs.transpose(1, 0, 2, 3).reshape(head_groups, whole_span, HEAD_SIZE)
    maxima = maxima.transpose(1, 0, 2).reshape(head_groups, whole_span)
    sums = sums.transpose(1, 0, 2).reshape(head_groups, whole_span)
    return (outputs, maxima, sums)

def attend_backward(group_queries, group_keys, group_values, group_gradient, maxima, sums, key_reach):
    whole_span = group_keys.shape[0]
    padded_keys, key_span = padded_window(group_keys)
    padded_values, key_span = padded_window(group_values)
    empty = jnp.zeros((key_span + whole_span, HEAD_SIZE), jnp.float32)

    def one_block(carry, block_index):
        key_accumulator, value_accumulator = carry
        first_query = block_index * SEQUENCE_SHARD
        query_block = lax.dynamic_slice_in_dim(group_queries, first_query, SEQUENCE_SHARD, 1)
        grad_rows = lax.dynamic_slice_in_dim(group_gradient, first_query, SEQUENCE_SHARD, 1)
        block_max = lax.dynamic_slice_in_dim(maxima, first_query, SEQUENCE_SHARD, 1)
        block_sum = lax.dynamic_slice_in_dim(sums, first_query, SEQUENCE_SHARD, 1)
        key_row_block = lax.dynamic_slice_in_dim(padded_keys, first_query, key_span + SEQUENCE_SHARD, 0)
        value_rows = lax.dynamic_slice_in_dim(padded_values, first_query, key_span + SEQUENCE_SHARD, 0)
        logits, scaling = masked_logits(query_block, key_row_block, first_query, key_reach)
        probs = jnp.exp(logits - block_max[..., None]) / block_sum[..., None]
        weights = probs.astype(jnp.bfloat16)
        prob_grad = jnp.einsum('gsd,kd->gsk', grad_rows.astype(jnp.float32), value_rows.astype(jnp.float32))
        row_delta = lax.optimization_barrier(jnp.sum(probs * prob_grad, axis=-1, keepdims=True))
        logit_grad = (probs * (prob_grad - row_delta) * scaling).astype(jnp.bfloat16)
        query_grad = jnp.einsum('gsk,kd->gsd', logit_grad.astype(jnp.float32), key_row_block.astype(jnp.float32))
        key_part = jnp.einsum('gsk,gsd->kd', logit_grad.astype(jnp.float32), query_block.astype(jnp.float32))
        value_part = jnp.einsum('gsk,gsd->kd', weights.astype(jnp.float32), grad_rows.astype(jnp.float32))
        old_keys = lax.dynamic_slice_in_dim(key_accumulator, first_query, key_span + SEQUENCE_SHARD, 0)
        old_values = lax.dynamic_slice_in_dim(value_accumulator, first_query, key_span + SEQUENCE_SHARD, 0)
        key_accumulator = lax.dynamic_update_slice_in_dim(key_accumulator, old_keys + key_part, first_query, 0)
        value_accumulator = lax.dynamic_update_slice_in_dim(value_accumulator, old_values + value_part, first_query, 0)
        return ((key_accumulator, value_accumulator), query_grad)
    (key_accumulator, value_accumulator), query_parts = lax.scan(one_block, (empty, empty), jnp.arange(whole_span // SEQUENCE_SHARD, dtype=jnp.int32))
    head_groups = group_queries.shape[0]
    query_parts = query_parts.transpose(1, 0, 2, 3).reshape(head_groups, whole_span, HEAD_SIZE)
    return (query_parts, key_accumulator[key_span:], value_accumulator[key_span:])

def decay_weights(block_queries, block_keys, cumulative):
    block_rows = cumulative.shape[0]
    lower_mask = jnp.arange(block_rows)[:, None] >= jnp.arange(block_rows)[None, :]
    gaps = jnp.where(lower_mask, cumulative[:, None] - cumulative[None, :], 0.0)
    products = jnp.dot(block_queries, block_keys.T, preferred_element_type=jnp.float32)
    return jnp.where(lower_mask, jnp.exp(gaps), 0.0) * products

def membrane_forward(head_queries, head_keys, head_spikes, decay_row):
    count = head_keys.shape[0] // SEQUENCE_SHARD
    stacked = (head_queries.reshape(count, SEQUENCE_SHARD, HEAD_SIZE), head_keys.reshape(count, SEQUENCE_SHARD, HEAD_SIZE), head_spikes.reshape(count, SEQUENCE_SHARD, HEAD_SIZE), decay_row.reshape(count, SEQUENCE_SHARD))

    def one_block(state, divided_slices):
        block_queries, block_keys, block_spikes, block_logs = divided_slices
        cumulative = jnp.cumsum(block_logs)
        decayed = decay_weights(block_queries, block_keys, cumulative)
        spike_float = block_spikes.astype(jnp.float32)
        carried = jnp.dot(block_queries.astype(jnp.float32), state, precision=precise)
        result = jnp.dot(decayed, spike_float, precision=precise) + jnp.exp(cumulative)[:, None] * carried
        weighted = block_keys.astype(jnp.float32) * jnp.exp(cumulative[-1] - cumulative)[:, None]
        state = jnp.exp(cumulative[-1]) * state + jnp.dot(weighted.T, spike_float, precision=precise)
        return (state, result)
    _, results = lax.scan(one_block, jnp.zeros((HEAD_SIZE, HEAD_SIZE), jnp.float32), stacked)
    return results.reshape(count * SEQUENCE_SHARD, HEAD_SIZE)

def membrane_backward(head_queries, head_keys, decay_row, head_grads):
    count = head_keys.shape[0] // SEQUENCE_SHARD
    stacked = (head_queries.reshape(count, SEQUENCE_SHARD, HEAD_SIZE), head_keys.reshape(count, SEQUENCE_SHARD, HEAD_SIZE), decay_row.reshape(count, SEQUENCE_SHARD), head_grads.reshape(count, SEQUENCE_SHARD, HEAD_SIZE))

    def one_block(carry, divided_slices):
        block_queries, block_keys, block_logs, block_grads = divided_slices
        cumulative = jnp.cumsum(block_logs)
        decayed = decay_weights(block_queries, block_keys, cumulative)
        later = jnp.dot(block_keys.astype(jnp.float32), carry, precision=precise)
        result = jnp.dot(decayed.T, block_grads, precision=precise) + jnp.exp(cumulative[-1] - cumulative)[:, None] * later
        weighted = block_queries.astype(jnp.float32) * jnp.exp(cumulative)[:, None]
        carry = jnp.dot(weighted.T, block_grads, precision=precise) + jnp.exp(cumulative[-1]) * carry
        return (carry, result)
    _, results = lax.scan(one_block, jnp.zeros((HEAD_SIZE, HEAD_SIZE), jnp.float32), stacked, reverse=True)
    return results.reshape(count * SEQUENCE_SHARD, HEAD_SIZE)

def reference(attention_queries, attention_keys, attention_values, key_window_length, norm_gain, spike_levels, lin_queries, lin_keys, decay_logs, cotangent):
    batch_count, whole_span, width_all = attention_queries.shape
    head_groups = TEST_LANES // KEY_VALUE_HEADS
    query_block = attention_queries.reshape(batch_count, whole_span, KEY_VALUE_HEADS, head_groups, HEAD_SIZE).transpose(0, 2, 3, 1, 4)
    key_head_rows = attention_keys.reshape(batch_count, whole_span, KEY_VALUE_HEADS, HEAD_SIZE).transpose(0, 2, 1, 3)
    value_head_rows = attention_values.reshape(batch_count, whole_span, KEY_VALUE_HEADS, HEAD_SIZE).transpose(0, 2, 1, 3)
    window_reaches = jnp.broadcast_to(key_window_length[None, :], (batch_count, KEY_VALUE_HEADS))
    outputs, maxima, sums = jax.vmap(jax.vmap(attend_forward))(query_block, key_head_rows, value_head_rows, window_reaches)
    out_float = outputs.reshape(batch_count, TEST_LANES, whole_span, HEAD_SIZE).astype(jnp.float32)
    mean_square = lax.optimization_barrier(jnp.sum(out_float * out_float, axis=(1, 3))) / width_all
    inverse = 1.0 / jnp.sqrt(mean_square + epsilon)
    normed = out_float * inverse[:, None, :, None]
    gain_rows = norm_gain.reshape(TEST_LANES, HEAD_SIZE)[None, :, None, :]
    ceiling = spike_levels.astype(jnp.float32).reshape(TEST_LANES, HEAD_SIZE)[None, :, None, :]
    bounded = jnp.tanh(normed * gain_rows / ceiling)
    spikes = (ceiling * bounded).astype(jnp.bfloat16)
    membrane_queries = lin_queries.reshape(batch_count, whole_span, TEST_LANES, HEAD_SIZE).transpose(0, 2, 1, 3)
    membrane_keys = lin_keys.reshape(batch_count, whole_span, TEST_LANES, HEAD_SIZE).transpose(0, 2, 1, 3)
    membrane = jax.vmap(jax.vmap(membrane_forward))(membrane_queries, membrane_keys, spikes, decay_logs)
    scale_out = 1.0 / jnp.sqrt(lax.optimization_barrier(jnp.mean(membrane * membrane, axis=-1)) + epsilon)
    unit_out = membrane * scale_out[..., None]
    layer_output = unit_out.astype(jnp.bfloat16).transpose(0, 2, 1, 3).reshape(batch_count, whole_span, width_all)
    incoming = cotangent.reshape(batch_count, whole_span, TEST_LANES, HEAD_SIZE).transpose(0, 2, 1, 3).astype(jnp.float32)
    membrane_grad = scale_out[..., None] * (incoming - unit_out * lax.optimization_barrier(jnp.mean(incoming * unit_out, axis=-1, keepdims=True)))
    spike_grad = jax.vmap(jax.vmap(membrane_backward))(membrane_queries, membrane_keys, decay_logs, membrane_grad)
    level_grad = spike_grad * (1.0 - bounded * bounded)
    gain_grads = lax.optimization_barrier(jnp.sum(level_grad * normed, axis=(0, 2))).reshape(width_all)
    normed_grad = level_grad * gain_rows
    slope_sum = lax.optimization_barrier(jnp.sum(normed_grad * normed, axis=(1, 3))) / width_all
    output_gradient = (inverse[:, None, :, None] * (normed_grad - normed * slope_sum[:, None, :, None])).astype(jnp.bfloat16)
    group_gradient = output_gradient.reshape(batch_count, KEY_VALUE_HEADS, head_groups, whole_span, HEAD_SIZE)
    query_parts, key_accumulator, value_accumulator = jax.vmap(jax.vmap(attend_backward))(query_block, key_head_rows, value_head_rows, group_gradient, maxima, sums, window_reaches)
    query_grads = query_parts.astype(jnp.bfloat16).transpose(0, 3, 1, 2, 4).reshape(batch_count, whole_span, width_all)
    key_gradient = key_accumulator.astype(jnp.bfloat16).transpose(0, 2, 1, 3).reshape(batch_count, whole_span, KEY_VALUE_HEADS * HEAD_SIZE)
    value_gradient = value_accumulator.astype(jnp.bfloat16).transpose(0, 2, 1, 3).reshape(batch_count, whole_span, KEY_VALUE_HEADS * HEAD_SIZE)
    return (layer_output, query_grads, key_gradient, value_gradient, gain_grads)
```

```python
import functools
import math

import jax
import jax.numpy as jnp
from jax import lax
from jax.experimental import pallas as pl
from jax.experimental.pallas import tpu as pltpu
from jax.sharding import PartitionSpec as P

HEAD_SIZE = 128
D = 3584
LONGEST_WINDOW = 512

MESH = pl.DeviceIdType.MESH
f32 = jnp.float32
bf16 = jnp.bfloat16
precise = lax.Precision.HIGHEST
epsilon = 1e-06


def nn(left, right):
    return lax.dot_general(left, right, (((1,), (0,)), ((), ())), preferred_element_type=f32)


def nt(left, right):
    return lax.dot_general(left, right, (((1,), (1,)), ((), ())), preferred_element_type=f32)


def turned(block):
    return block.astype(f32).T


def kernel(
    sizes,
    q_ref,
    k_ref,
    v_ref,
    window_ref,
    gain_ref,
    level_ref,
    lq_ref,
    lk_ref,
    decay_ref,
    ct_ref,
    out_ref,
    qg_ref,
    kg_ref,
    vg_ref,
    gg_ref,
    pair_prev,
    probs,
    heads_out,
    decayed,
    ct_turned,
    gain_cols,
    level_cols,
    bounded_buf,
    spikes_buf,
    work,
    out_grads,
    logit_grads,
    weights_buf,
    part_one,
    part_two,
    square_slots,
    slope_slots,
    state_out,
    state_in,
    after_out,
    after_in,
    gain_slots,
    gain_sum_slots,
    pair_out,
    pair_in,
    pair_send,
    pair_recv,
    square_send,
    square_recv,
    state_send,
    state_recv,
    after_send,
    after_recv,
    slope_send,
    slope_recv,
    dp_send,
    dp_recv,
    seq_send,
    seq_recv,
    grad_send,
    grad_recv,
):
    n_seq, n_dp, n_tensor, previous, heads = sizes
    seq, dp, ten = lax.axis_index("seq"), lax.axis_index("dp"), lax.axis_index("tensor")
    size = HEAD_SIZE
    scaling = 1.0 / math.sqrt(HEAD_SIZE)
    cols = [slice(h * size, (h + 1) * size) for h in range(heads)]

    barrier = pltpu.get_barrier_semaphore()
    for axis, me, count in (("seq", seq, n_seq), ("dp", dp, n_dp), ("tensor", ten, n_tensor)):
        for step in range(1, count):
            pl.semaphore_signal(
                barrier,
                inc=1,
                device_id={axis: lax.rem(me + step, count)},
                device_id_type=MESH,
            )
    pl.semaphore_wait(barrier, n_seq + n_dp + n_tensor - 3)

    def remote(src, dst, send, recv, axis, target):
        return pltpu.make_async_remote_copy(
            src_ref=src,
            dst_ref=dst,
            send_sem=send,
            recv_sem=recv,
            device_id={axis: target},
            device_id_type=MESH,
        )

    def exchange(slots, send, recv, axis, me, count):
        def start():
            for step in range(1, count):
                remote(
                    slots.at[me],
                    slots.at[me],
                    send.at[step - 1],
                    recv.at[me],
                    axis,
                    lax.rem(me + step, count),
                ).start()

        def wait():
            for step in range(1, count):
                sender = lax.rem(me + count - step, count)
                copy = remote(
                    slots.at[me], slots.at[sender], send.at[step - 1], recv.at[sender], axis, sender
                )
                copy.wait_recv()

        def drain():
            for step in range(1, count):
                remote(
                    slots.at[me],
                    slots.at[me],
                    send.at[step - 1],
                    recv.at[me],
                    axis,
                    lax.rem(me + step, count),
                ).wait_send()

        return start, wait, drain

    def pair_copy(index, distance):
        source = (k_ref, v_ref)[index].at[0]
        return remote(
            source,
            pair_prev.at[index, distance - 1],
            pair_send.at[index, distance - 1],
            pair_recv.at[index, distance - 1],
            "seq",
            lax.rem(seq + distance, n_seq),
        )

    def grad_copy(index, distance):
        return remote(
            pair_out.at[index, distance - 1],
            pair_in.at[index, distance - 1],
            grad_send.at[index, distance - 1],
            grad_recv.at[index, distance - 1],
            "seq",
            lax.rem(seq + n_seq - distance, n_seq),
        )

    for distance in range(1, previous + 1):

        @pl.when(seq + distance < n_seq)
        def _():
            pair_copy(0, distance).start()
            pair_copy(1, distance).start()

        @pl.when(seq < distance)
        def _():
            for index in range(2):
                pair_prev[index, distance - 1] = jnp.zeros((size, size), bf16)

    row_index = lax.broadcasted_iota(jnp.int32, (size, size), 0)
    column_index = lax.broadcasted_iota(jnp.int32, (size, size), 1)
    causal = row_index <= column_index
    window = window_ref[0]
    keys = k_ref[0]
    values = v_ref[0]
    keys_turned = turned(keys).astype(bf16)
    values_turned = turned(values).astype(bf16)

    for h in range(heads):
        scores = nt(keys, q_ref[0, :, cols[h]]) * scaling
        probs[0, h] = jnp.where(causal, scores, -jnp.inf)

    def attend(blocks):
        squares = jnp.zeros((size, size), f32)
        block_keys = [pair_prev[0, d] for d in range(blocks)]
        block_values = [turned(pair_prev[1, d]).astype(bf16) for d in range(blocks)]
        masks = []
        for d in range(blocks):
            seen = (d + 1) * size + column_index - row_index < window
            masks.append(seen & (seq > d) if n_seq > 2 else seen)
        for h in range(heads):
            scores = [probs[0, h]]
            for d in range(blocks):
                score = nt(block_keys[d], q_ref[0, :, cols[h]]) * scaling
                scores.append(jnp.where(masks[d], score, -jnp.inf))
            top = functools.reduce(
                jnp.maximum, [jnp.max(score, axis=0, keepdims=True) for score in scores]
            )
            exponents = [jnp.exp(score - top) for score in scores]
            total = sum(jnp.sum(exponent, axis=0, keepdims=True) for exponent in exponents)
            share = 1.0 / total
            result = None
            for d, exponent in enumerate(exponents):
                prob = exponent * share
                probs[d, h] = prob
                weights = prob.astype(bf16)
                weights_buf[d, :, cols[h]] = weights
                part = nn(values_turned if d == 0 else block_values[d - 1], weights)
                result = part if result is None else result + part
            result = result.astype(bf16).astype(f32)
            heads_out[h] = result
            squares = squares + result * result
        part_one[...] = jnp.broadcast_to(jnp.sum(squares, axis=0, keepdims=True), (8, size))

    @pl.when(seq == 0)
    def _():
        attend(0)

    if previous:

        @pl.when(seq > 0)
        def _():
            for distance in range(1, previous + 1):

                @pl.when(seq >= distance)
                def _():
                    pair_copy(0, distance).wait_recv()
                    pair_copy(1, distance).wait_recv()

            attend(previous)

    square_slots[ten] = part_one[...]
    start, wait_squares, drain_squares = exchange(
        square_slots, square_send, square_recv, "tensor", ten, n_tensor
    )
    start()

    logs = decay_ref[0]
    upper = jnp.where(causal, 1.0, 0.0)
    cumulative = jnp.dot(logs, upper, precision=precise, preferred_element_type=f32)
    whole = jnp.dot(
        logs, jnp.ones((size, size), f32), precision=precise, preferred_element_type=f32
    )
    tail = jnp.exp(jnp.minimum(whole - cumulative, 0.0))
    grown = jnp.exp(cumulative)
    block_decay = jnp.exp(whole)
    for h in range(heads):
        level_rows = jnp.broadcast_to(level_ref[h : h + 1, :].astype(f32), (size, size))
        gain_rows = jnp.broadcast_to(gain_ref[h : h + 1, :], (size, size))
        level_cols[h] = level_rows.T
        gain_cols[h] = gain_rows.T
        ct_turned[h] = turned(ct_ref[0, :, cols[h]])
        along = jnp.broadcast_to(cumulative[h : h + 1, :], (size, size))
        gaps = jnp.where(causal, along - along.T, -jnp.inf)
        product = nt(lk_ref[0, :, cols[h]], lq_ref[0, :, cols[h]])
        decayed[h] = (jnp.exp(gaps) * product).astype(bf16)

    wait_squares()
    square_sum = sum(square_slots[i] for i in range(n_tensor))[:1]
    inverse = 1.0 / jnp.sqrt(square_sum / D + epsilon)

    def state_copy(h):
        return remote(
            state_out.at[h],
            state_in.at[h],
            state_send.at[h],
            state_recv.at[h],
            "seq",
            lax.rem(seq + 1, n_seq),
        )

    def after_copy(h):
        return remote(
            after_out.at[h],
            after_in.at[h],
            after_send.at[h],
            after_recv.at[h],
            "seq",
            lax.rem(seq + n_seq - 1, n_seq),
        )

    for h in range(heads):
        normed = heads_out[h] * inverse
        heads_out[h] = normed
        bounded = jnp.tanh(normed * gain_cols[h] / level_cols[h])
        bounded_buf[h] = bounded
        spikes = (level_cols[h] * bounded).astype(bf16)
        spikes_buf[h] = spikes
        fading = (spikes.astype(f32) * tail[h : h + 1]).astype(bf16)
        state_out[h] = nn(fading, lk_ref[0, :, cols[h]]).astype(state_out.dtype)
        if n_seq == 2:

            @pl.when(seq == 0)
            def _():
                state_copy(h).start()

    for h in range(heads):
        work[h] = nn(spikes_buf[h], decayed[h])

    if n_seq > 2:

        @pl.when(seq == 0)
        def _():
            for h in range(heads):
                state_copy(h).start()

    if n_seq > 1:

        @pl.when(seq > 0)
        def _():
            for h in range(heads):
                state_copy(h).wait_recv()
                if n_seq > 2:
                    state_out[h] = (
                        block_decay[h : h + 1] * state_in[h].astype(f32) + state_out[h].astype(f32)
                    ).astype(state_out.dtype)

                    @pl.when(seq < n_seq - 1)
                    def _():
                        state_copy(h).start()

            for h in range(heads):
                carried = nt(state_in[h].astype(bf16), lq_ref[0, :, cols[h]])
                work[h] = work[h] + grown[h : h + 1] * carried

    for h in range(heads):
        membrane = work[h]
        mean = jnp.sum(membrane * membrane, axis=0, keepdims=True) / size
        scale = 1.0 / jnp.sqrt(mean + epsilon)
        unit = membrane * scale
        incoming = ct_turned[h]
        inner = jnp.sum(incoming * unit, axis=0, keepdims=True) / size
        grad = scale * (incoming - unit * inner)
        work[h] = unit
        spikes_buf[h] = grad.astype(bf16)
        after_out[h] = nn((grad * grown[h : h + 1]).astype(bf16), lq_ref[0, :, cols[h]]).astype(
            after_out.dtype
        )
        if n_seq == 2:

            @pl.when(seq == 1)
            def _():
                after_copy(h).start()

    if n_seq > 2:

        @pl.when(seq == n_seq - 1)
        def _():
            for h in range(heads):
                after_copy(h).start()

    for h in range(heads):
        out_ref[0, :, cols[h]] = work[h].T.astype(bf16)
        work[h] = nt(spikes_buf[h], decayed[h])

    if n_seq > 1:

        @pl.when(seq < n_seq - 1)
        def _():
            for h in range(heads):
                after_copy(h).wait_recv()
                if n_seq > 2:
                    after_out[h] = (
                        block_decay[h : h + 1] * after_in[h].astype(f32) + after_out[h].astype(f32)
                    ).astype(after_out.dtype)

                    @pl.when(seq > 0)
                    def _():
                        after_copy(h).start()

            for h in range(heads):
                later = nt(after_in[h].astype(bf16), lk_ref[0, :, cols[h]])
                work[h] = work[h] + tail[h : h + 1] * later

    slope_part = jnp.zeros((size, size), f32)
    for h in range(heads):
        bounded = bounded_buf[h]
        level_grad = work[h] * (1.0 - bounded * bounded)
        with_normed = level_grad * heads_out[h]
        work[h] = level_grad
        bounded_buf[h] = with_normed
        slope_part = slope_part + with_normed * gain_cols[h]
    part_two[...] = jnp.broadcast_to(jnp.sum(slope_part, axis=0, keepdims=True), (8, size))
    slope_slots[ten] = part_two[...]
    start, wait_slopes, drain_slopes = exchange(
        slope_slots, slope_send, slope_recv, "tensor", ten, n_tensor
    )
    start()

    rows = [jnp.sum(bounded_buf[h].T, axis=0, keepdims=True) for h in range(heads)]
    rows.append(jnp.zeros((8 - heads, size), f32))
    gain_slots[dp] = jnp.concatenate(rows, axis=0)
    start, wait_dp, drain_dp = exchange(gain_slots, dp_send, dp_recv, "dp", dp, n_dp)
    start()

    wait_slopes()
    slope = sum(slope_slots[i] for i in range(n_tensor))[:1] / D
    for h in range(heads):
        normed_grad = work[h] * gain_cols[h]
        out_grads[:, cols[h]] = (inverse * (normed_grad - heads_out[h] * slope)).astype(bf16)

    def back(blocks):
        block_values = [values] + [pair_prev[1, d] for d in range(blocks)]
        for h in range(heads):
            prob_grads = [nn(block, out_grads[:, cols[h]]) for block in block_values]
            delta = sum(
                jnp.sum(probs[d, h] * prob_grad, axis=0, keepdims=True)
                for d, prob_grad in enumerate(prob_grads)
            )
            for d, prob_grad in enumerate(prob_grads):
                logit_grad = probs[d, h] * (prob_grad - delta) * scaling
                logit_grads[d, :, cols[h]] = logit_grad.astype(bf16)

    def pair_sums(d):
        key_sum = sum(nn(logit_grads[d, :, cols[h]], q_ref[0, :, cols[h]]) for h in range(heads))
        value_sum = nt(weights_buf[d], out_grads[...])
        return key_sum, value_sum

    @pl.when(seq == 0)
    def _():
        back(0)

    if previous:

        @pl.when(seq > 0)
        def _():
            back(previous)
            for distance in range(1, previous + 1):
                key_sum, value_sum = pair_sums(distance)
                pair_out[0, distance - 1] = key_sum
                pair_out[1, distance - 1] = value_sum

                @pl.when(seq >= distance)
                def _():
                    grad_copy(0, distance).start()
                    grad_copy(1, distance).start()

    wait_dp()
    gain_sum_slots[seq] = sum(gain_slots[i] for i in range(n_dp))
    start, wait_seq, drain_seq = exchange(gain_sum_slots, seq_send, seq_recv, "seq", seq, n_seq)
    start()

    @pl.when(seq == 0)
    def _():
        for h in range(heads):
            query_grad = nn(keys_turned, logit_grads[0, :, cols[h]])
            qg_ref[0, :, cols[h]] = query_grad.T.astype(bf16)

    if previous:

        @pl.when(seq > 0)
        def _():
            earlier = [turned(pair_prev[0, d]).astype(bf16) for d in range(previous)]
            for h in range(heads):
                query_grad = nn(keys_turned, logit_grads[0, :, cols[h]])
                for d in range(previous):
                    query_grad = query_grad + nn(earlier[d], logit_grads[d + 1, :, cols[h]])
                qg_ref[0, :, cols[h]] = query_grad.T.astype(bf16)

    key_sum, value_sum = pair_sums(0)
    pair_out[0, previous] = key_sum
    pair_out[1, previous] = value_sum
    wait_seq()
    gg_ref[...] = sum(gain_sum_slots[i] for i in range(n_seq))[:heads]

    for distance in range(1, previous + 1):

        @pl.when(seq + distance < n_seq)
        def _():
            for index in range(2):
                grad_copy(index, distance).wait_recv()
                pair_out[index, previous] = (
                    pair_out[index, previous] + pair_in[index, distance - 1]
                )

    kg_ref[0] = pair_out[0, previous].astype(bf16)
    vg_ref[0] = pair_out[1, previous].astype(bf16)

    for distance in range(1, previous + 1):

        @pl.when(seq + distance < n_seq)
        def _():
            pair_copy(0, distance).wait_send()
            pair_copy(1, distance).wait_send()

        @pl.when(seq >= distance)
        def _():
            grad_copy(0, distance).wait_send()
            grad_copy(1, distance).wait_send()

    if n_seq > 1:

        @pl.when(seq < n_seq - 1)
        def _():
            for h in range(heads):
                state_copy(h).wait_send()

        @pl.when(seq > 0)
        def _():
            for h in range(heads):
                after_copy(h).wait_send()

    drain_squares()
    drain_slopes()
    drain_dp()
    drain_seq()


def local(
    attention_queries,
    attention_keys,
    attention_values,
    key_window_length,
    norm_gain,
    spike_levels,
    lin_queries,
    lin_keys,
    decay_logs,
    cotangent,
):
    n_seq, n_dp, n_tensor = (lax.axis_size(axis) for axis in ("seq", "dp", "tensor"))
    rows = attention_queries.shape[1]
    heads = attention_queries.shape[2] // HEAD_SIZE
    previous = min((LONGEST_WINDOW + rows - 1) // rows, n_seq - 1)
    slots = max(previous, 1)
    state_type = bf16 if n_seq == 2 else f32
    size = HEAD_SIZE
    vmem = pl.BlockSpec(memory_space=pltpu.VMEM)
    smem = pl.BlockSpec(memory_space=pltpu.SMEM)
    tiles = (heads, size, size)
    dma = pltpu.SemaphoreType.DMA
    outputs = (
        jax.ShapeDtypeStruct(attention_queries.shape, bf16),
        jax.ShapeDtypeStruct(attention_queries.shape, bf16),
        jax.ShapeDtypeStruct(attention_keys.shape, bf16),
        jax.ShapeDtypeStruct(attention_keys.shape, bf16),
        jax.ShapeDtypeStruct((heads, size), f32),
    )
    scratch = [
        pltpu.VMEM((2, slots, size, size), bf16),
        pltpu.VMEM((previous + 1,) + tiles, f32),
        pltpu.VMEM(tiles, f32),
        pltpu.VMEM(tiles, bf16),
        pltpu.VMEM(tiles, f32),
        pltpu.VMEM(tiles, f32),
        pltpu.VMEM(tiles, f32),
        pltpu.VMEM(tiles, f32),
        pltpu.VMEM(tiles, bf16),
        pltpu.VMEM(tiles, f32),
        pltpu.VMEM((size, heads * size), bf16),
        pltpu.VMEM((previous + 1, size, heads * size), bf16),
        pltpu.VMEM((previous + 1, size, heads * size), bf16),
        pltpu.VMEM((8, size), f32),
        pltpu.VMEM((8, size), f32),
        pltpu.VMEM((n_tensor, 8, size), f32),
        pltpu.VMEM((n_tensor, 8, size), f32),
        pltpu.VMEM(tiles, state_type),
        pltpu.VMEM(tiles, state_type),
        pltpu.VMEM(tiles, state_type),
        pltpu.VMEM(tiles, state_type),
        pltpu.VMEM((n_dp, 8, size), f32),
        pltpu.VMEM((n_seq, 8, size), f32),
        pltpu.VMEM((2, previous + 1, size, size), f32),
        pltpu.VMEM((2, slots, size, size), f32),
        dma((2, slots)),
        dma((2, slots)),
        dma((n_tensor,)),
        dma((n_tensor,)),
        dma((heads,)),
        dma((heads,)),
        dma((heads,)),
        dma((heads,)),
        dma((n_tensor,)),
        dma((n_tensor,)),
        dma((n_dp,)),
        dma((n_dp,)),
        dma((n_seq,)),
        dma((n_seq,)),
        dma((2, slots)),
        dma((2, slots)),
    ]
    layer_output, query_grads, key_gradient, value_gradient, gain_grads = pl.pallas_call(
        functools.partial(kernel, (n_seq, n_dp, n_tensor, previous, heads)),
        out_shape=outputs,
        in_specs=[vmem, vmem, vmem, smem] + [vmem] * 6,
        out_specs=(vmem,) * 5,
        scratch_shapes=scratch,
        compiler_params=pltpu.CompilerParams(
            collective_id=0, has_side_effects=True, vmem_limit_bytes=40 * 1024 * 1024
        ),
        name="layer_pair",
    )(
        attention_queries,
        attention_keys,
        attention_values,
        key_window_length,
        norm_gain.reshape(heads, size),
        spike_levels.reshape(heads, size),
        lin_queries,
        lin_keys,
        decay_logs,
        cotangent,
    )
    return (layer_output, query_grads, key_gradient, value_gradient, gain_grads.reshape(-1))


def solution(mesh):
    placed = (
        P("dp", "seq", "tensor"),
        P("dp", "seq", "tensor"),
        P("dp", "seq", "tensor"),
        P("tensor"),
        P("tensor"),
        P("tensor"),
        P("dp", "seq", "tensor"),
        P("dp", "seq", "tensor"),
        P("dp", "tensor", "seq"),
        P("dp", "seq", "tensor"),
    )
    return jax.shard_map(
        local,
        mesh=mesh,
        in_specs=placed,
        out_specs=(
            P("dp", "seq", "tensor"),
            P("dp", "seq", "tensor"),
            P("dp", "seq", "tensor"),
            P("dp", "seq", "tensor"),
            P("tensor"),
        ),
        check_vma=False,
    )
```

```python
import functools
import math

import jax
import jax.numpy as jnp
from jax import lax
from jax.experimental import pallas as pl
from jax.experimental.pallas import tpu as pltpu
from jax.sharding import PartitionSpec as P

HEAD_SIZE = 128
D = 3584
LONGEST_WINDOW = 512
VMEM_LIMIT = 63 * 1024 * 1024

MESH = pl.DeviceIdType.MESH
f32 = jnp.float32
bf16 = jnp.bfloat16
precise = lax.Precision.HIGHEST
epsilon = 1e-06


def nn(left, right):
    return lax.dot_general(left, right, (((1,), (0,)), ((), ())), preferred_element_type=f32)


def nt(left, right):
    return lax.dot_general(left, right, (((1,), (1,)), ((), ())), preferred_element_type=f32)


def turned(block):
    return block.astype(f32).T


def kernel(
    sizes,
    q_hbm,
    k_hbm,
    v_hbm,
    window_ref,
    gain_hbm,
    level_hbm,
    lq_hbm,
    lk_hbm,
    decay_hbm,
    ct_hbm,
    out_hbm,
    qg_hbm,
    kg_hbm,
    vg_hbm,
    gg_hbm,
    out_ref,
    qg_ref,
    kg_ref,
    vg_ref,
    gg_ref,
    store_sems,
    q_ref,
    k_ref,
    v_ref,
    gain_ref,
    level_ref,
    lq_ref,
    lk_ref,
    decay_ref,
    ct_ref,
    fetch_sems,
    pair_prev,
    probs,
    heads_out,
    decayed,
    ct_turned,
    gain_cols,
    level_cols,
    bounded_buf,
    spikes_buf,
    work,
    out_grads,
    logit_grads,
    weights_buf,
    part_one,
    part_two,
    square_slots,
    slope_slots,
    state_out,
    state_in,
    after_out,
    after_in,
    gain_slots,
    gain_sum_slots,
    pair_out,
    pair_in,
    pair_send,
    pair_recv,
    square_send,
    square_recv,
    state_send,
    state_recv,
    after_send,
    after_recv,
    slope_send,
    slope_recv,
    dp_send,
    dp_recv,
    seq_send,
    seq_recv,
    grad_send,
    grad_recv,
):
    n_seq, n_dp, n_tensor, previous, heads = sizes
    seq, dp, ten = lax.axis_index("seq"), lax.axis_index("dp"), lax.axis_index("tensor")
    size = HEAD_SIZE
    scaling = 1.0 / math.sqrt(HEAD_SIZE)
    cols = [slice(h * size, (h + 1) * size) for h in range(heads)]

    barrier = pltpu.get_barrier_semaphore()
    for axis, me, count in (("seq", seq, n_seq), ("dp", dp, n_dp), ("tensor", ten, n_tensor)):
        for step in range(1, count):
            pl.semaphore_signal(
                barrier,
                inc=1,
                device_id={axis: lax.rem(me + step, count)},
                device_id_type=MESH,
            )
    fetches = [
        pltpu.make_async_copy(source, target, fetch_sems.at[i])
        for i, (source, target) in enumerate(
            (
                (k_hbm, k_ref),
                (q_hbm, q_ref),
                (v_hbm, v_ref),
                (decay_hbm, decay_ref),
                (gain_hbm, gain_ref),
                (level_hbm, level_ref),
                (lk_hbm, lk_ref),
                (lq_hbm, lq_ref),
                (ct_hbm, ct_ref),
            )
        )
    ]
    for fetch in fetches:
        fetch.start()
    stores = [
        pltpu.make_async_copy(source, target, store_sems.at[i])
        for i, (source, target) in enumerate(
            (
                (out_ref, out_hbm),
                (qg_ref, qg_hbm),
                (kg_ref, kg_hbm),
                (vg_ref, vg_hbm),
                (gg_ref, gg_hbm),
            )
        )
    ]
    pl.semaphore_wait(barrier, n_seq + n_dp + n_tensor - 3)

    def remote(src, dst, send, recv, axis, target):
        return pltpu.make_async_remote_copy(
            src_ref=src,
            dst_ref=dst,
            send_sem=send,
            recv_sem=recv,
            device_id={axis: target},
            device_id_type=MESH,
        )

    def exchange(slots, send, recv, axis, me, count):
        def start():
            for step in range(1, count):
                remote(
                    slots.at[me],
                    slots.at[me],
                    send.at[step - 1],
                    recv.at[me],
                    axis,
                    lax.rem(me + step, count),
                ).start()

        def wait():
            for step in range(1, count):
                sender = lax.rem(me + count - step, count)
                copy = remote(
                    slots.at[me], slots.at[sender], send.at[step - 1], recv.at[sender], axis, sender
                )
                copy.wait_recv()

        def drain():
            for step in range(1, count):
                remote(
                    slots.at[me],
                    slots.at[me],
                    send.at[step - 1],
                    recv.at[me],
                    axis,
                    lax.rem(me + step, count),
                ).wait_send()

        return start, wait, drain

    def pair_copy(index, distance):
        source = (k_hbm, v_hbm)[index].at[0]
        return remote(
            source,
            pair_prev.at[index, distance - 1],
            pair_send.at[index, distance - 1],
            pair_recv.at[index, distance - 1],
            "seq",
            lax.rem(seq + distance, n_seq),
        )

    def grad_copy(index, distance):
        return remote(
            pair_out.at[index, distance - 1],
            pair_in.at[index, distance - 1],
            grad_send.at[index, distance - 1],
            grad_recv.at[index, distance - 1],
            "seq",
            lax.rem(seq + n_seq - distance, n_seq),
        )

    for distance in range(1, previous + 1):

        @pl.when(seq + distance < n_seq)
        def _():
            pair_copy(0, distance).start()
            pair_copy(1, distance).start()

        @pl.when(seq < distance)
        def _():
            for index in range(2):
                pair_prev[index, distance - 1] = jnp.zeros((size, size), bf16)

    row_index = lax.broadcasted_iota(jnp.int32, (size, size), 0)
    column_index = lax.broadcasted_iota(jnp.int32, (size, size), 1)
    causal = row_index <= column_index
    window = window_ref[0]
    for fetch in fetches[:3]:
        fetch.wait()
    keys = k_ref[0]
    values = v_ref[0]
    keys_turned = turned(keys).astype(bf16)
    values_turned = turned(values).astype(bf16)

    for h in range(heads):
        scores = nt(keys, q_ref[0, :, cols[h]]) * scaling
        probs[0, h] = jnp.where(causal, scores, -jnp.inf)

    def attend(blocks):
        squares = jnp.zeros((size, size), f32)
        block_keys = [pair_prev[0, d] for d in range(blocks)]
        block_values = [turned(pair_prev[1, d]).astype(bf16) for d in range(blocks)]
        masks = []
        for d in range(blocks):
            seen = (d + 1) * size + column_index - row_index < window
            masks.append(seen & (seq > d) if n_seq > 2 else seen)
        for h in range(heads):
            scores = [probs[0, h]]
            for d in range(blocks):
                score = nt(block_keys[d], q_ref[0, :, cols[h]]) * scaling
                scores.append(jnp.where(masks[d], score, -jnp.inf))
            top = functools.reduce(
                jnp.maximum, [jnp.max(score, axis=0, keepdims=True) for score in scores]
            )
            exponents = [jnp.exp(score - top) for score in scores]
            total = sum(jnp.sum(exponent, axis=0, keepdims=True) for exponent in exponents)
            share = 1.0 / total
            result = None
            for d, exponent in enumerate(exponents):
                prob = exponent * share
                probs[d, h] = prob
                weights = prob.astype(bf16)
                weights_buf[d, :, cols[h]] = weights
                part = nn(values_turned if d == 0 else block_values[d - 1], weights)
                result = part if result is None else result + part
            result = result.astype(bf16).astype(f32)
            heads_out[h] = result
            squares = squares + result * result
        part_one[...] = jnp.broadcast_to(jnp.sum(squares, axis=0, keepdims=True), (8, size))

    @pl.when(seq == 0)
    def _():
        attend(0)

    if previous:

        @pl.when(seq > 0)
        def _():
            for distance in range(1, previous + 1):

                @pl.when(seq >= distance)
                def _():
                    pair_copy(0, distance).wait_recv()
                    pair_copy(1, distance).wait_recv()

            attend(previous)

    square_slots[ten] = part_one[...]
    start, wait_squares, drain_squares = exchange(
        square_slots, square_send, square_recv, "tensor", ten, n_tensor
    )
    start()

    for fetch in fetches[3:]:
        fetch.wait()
    logs = decay_ref[:, 0, :]
    upper = jnp.where(causal, 1.0, 0.0)
    cumulative = jnp.dot(logs, upper, precision=precise, preferred_element_type=f32)
    whole = jnp.dot(
        logs, jnp.ones((size, size), f32), precision=precise, preferred_element_type=f32
    )
    tail = jnp.exp(jnp.minimum(whole - cumulative, 0.0))
    grown = jnp.exp(cumulative)
    block_decay = jnp.exp(whole)
    for h in range(heads):
        level_rows = jnp.broadcast_to(level_ref[h : h + 1, :].astype(f32), (size, size))
        gain_rows = jnp.broadcast_to(gain_ref[h : h + 1, :], (size, size))
        level_cols[h] = level_rows.T
        gain_cols[h] = gain_rows.T
        ct_turned[h] = turned(ct_ref[0, :, cols[h]])
        along = jnp.broadcast_to(cumulative[h : h + 1, :], (size, size))
        gaps = jnp.where(causal, along - along.T, -jnp.inf)
        product = nt(lk_ref[0, :, cols[h]], lq_ref[0, :, cols[h]])
        decayed[h] = (jnp.exp(gaps) * product).astype(bf16)

    wait_squares()
    square_sum = sum(square_slots[i] for i in range(n_tensor))[:1]
    inverse = 1.0 / jnp.sqrt(square_sum / D + epsilon)

    def state_copy(h):
        return remote(
            state_out.at[h],
            state_in.at[h],
            state_send.at[h],
            state_recv.at[h],
            "seq",
            lax.rem(seq + 1, n_seq),
        )

    def after_copy(h):
        return remote(
            after_out.at[h],
            after_in.at[h],
            after_send.at[h],
            after_recv.at[h],
            "seq",
            lax.rem(seq + n_seq - 1, n_seq),
        )

    for h in range(heads):
        normed = heads_out[h] * inverse
        heads_out[h] = normed
        bounded = jnp.tanh(normed * gain_cols[h] / level_cols[h])
        bounded_buf[h] = bounded
        spikes = (level_cols[h] * bounded).astype(bf16)
        spikes_buf[h] = spikes
        fading = (spikes.astype(f32) * tail[h : h + 1]).astype(bf16)
        state_out[h] = nn(fading, lk_ref[0, :, cols[h]]).astype(state_out.dtype)
        if n_seq == 2:

            @pl.when(seq == 0)
            def _():
                state_copy(h).start()

    for h in range(heads):
        work[h] = nn(spikes_buf[h], decayed[h])

    if n_seq > 2:

        @pl.when(seq == 0)
        def _():
            for h in range(heads):
                state_copy(h).start()

    if n_seq > 1:

        @pl.when(seq > 0)
        def _():
            for h in range(heads):
                state_copy(h).wait_recv()
                if n_seq > 2:
                    state_out[h] = (
                        block_decay[h : h + 1] * state_in[h].astype(f32) + state_out[h].astype(f32)
                    ).astype(state_out.dtype)

                    @pl.when(seq < n_seq - 1)
                    def _():
                        state_copy(h).start()

            for h in range(heads):
                carried = nt(state_in[h].astype(bf16), lq_ref[0, :, cols[h]])
                work[h] = work[h] + grown[h : h + 1] * carried

    for h in range(heads):
        membrane = work[h]
        mean = jnp.sum(membrane * membrane, axis=0, keepdims=True) / size
        scale = 1.0 / jnp.sqrt(mean + epsilon)
        unit = membrane * scale
        incoming = ct_turned[h]
        inner = jnp.sum(incoming * unit, axis=0, keepdims=True) / size
        grad = scale * (incoming - unit * inner)
        work[h] = unit
        spikes_buf[h] = grad.astype(bf16)
        after_out[h] = nn((grad * grown[h : h + 1]).astype(bf16), lq_ref[0, :, cols[h]]).astype(
            after_out.dtype
        )
        if n_seq == 2:

            @pl.when(seq == 1)
            def _():
                after_copy(h).start()

    if n_seq > 2:

        @pl.when(seq == n_seq - 1)
        def _():
            for h in range(heads):
                after_copy(h).start()

    for h in range(heads):
        out_ref[0, :, cols[h]] = work[h].T.astype(bf16)
        work[h] = nt(spikes_buf[h], decayed[h])
    stores[0].start()

    if n_seq > 1:

        @pl.when(seq < n_seq - 1)
        def _():
            for h in range(heads):
                after_copy(h).wait_recv()
                if n_seq > 2:
                    after_out[h] = (
                        block_decay[h : h + 1] * after_in[h].astype(f32) + after_out[h].astype(f32)
                    ).astype(after_out.dtype)

                    @pl.when(seq > 0)
                    def _():
                        after_copy(h).start()

            for h in range(heads):
                later = nt(after_in[h].astype(bf16), lk_ref[0, :, cols[h]])
                work[h] = work[h] + tail[h : h + 1] * later

    slope_part = jnp.zeros((size, size), f32)
    for h in range(heads):
        bounded = bounded_buf[h]
        level_grad = work[h] * (1.0 - bounded * bounded)
        with_normed = level_grad * heads_out[h]
        work[h] = level_grad
        bounded_buf[h] = with_normed
        slope_part = slope_part + with_normed * gain_cols[h]
    part_two[...] = jnp.broadcast_to(jnp.sum(slope_part, axis=0, keepdims=True), (8, size))
    slope_slots[ten] = part_two[...]
    start, wait_slopes, drain_slopes = exchange(
        slope_slots, slope_send, slope_recv, "tensor", ten, n_tensor
    )
    start()

    rows = [jnp.sum(bounded_buf[h].T, axis=0, keepdims=True) for h in range(heads)]
    rows.append(jnp.zeros((8 - heads, size), f32))
    gain_slots[dp] = jnp.concatenate(rows, axis=0)
    start, wait_dp, drain_dp = exchange(gain_slots, dp_send, dp_recv, "dp", dp, n_dp)
    start()

    wait_slopes()
    slope = sum(slope_slots[i] for i in range(n_tensor))[:1] / D
    for h in range(heads):
        normed_grad = work[h] * gain_cols[h]
        out_grads[:, cols[h]] = (inverse * (normed_grad - heads_out[h] * slope)).astype(bf16)

    def back(blocks):
        block_values = [values] + [pair_prev[1, d] for d in range(blocks)]
        for h in range(heads):
            prob_grads = [nn(block, out_grads[:, cols[h]]) for block in block_values]
            delta = sum(
                jnp.sum(probs[d, h] * prob_grad, axis=0, keepdims=True)
                for d, prob_grad in enumerate(prob_grads)
            )
            for d, prob_grad in enumerate(prob_grads):
                logit_grad = probs[d, h] * (prob_grad - delta) * scaling
                logit_grads[d, :, cols[h]] = logit_grad.astype(bf16)

    def pair_sums(d):
        key_sum = sum(nn(logit_grads[d, :, cols[h]], q_ref[0, :, cols[h]]) for h in range(heads))
        value_sum = nt(weights_buf[d], out_grads[...])
        return key_sum, value_sum

    @pl.when(seq == 0)
    def _():
        back(0)

    if previous:

        @pl.when(seq > 0)
        def _():
            back(previous)
            for distance in range(1, previous + 1):
                key_sum, value_sum = pair_sums(distance)
                pair_out[0, distance - 1] = key_sum
                pair_out[1, distance - 1] = value_sum

                @pl.when(seq >= distance)
                def _():
                    grad_copy(0, distance).start()
                    grad_copy(1, distance).start()

    wait_dp()
    gain_sum_slots[seq] = sum(gain_slots[i] for i in range(n_dp))
    start, wait_seq, drain_seq = exchange(gain_sum_slots, seq_send, seq_recv, "seq", seq, n_seq)
    start()

    @pl.when(seq == 0)
    def _():
        for h in range(heads):
            query_grad = nn(keys_turned, logit_grads[0, :, cols[h]])
            qg_ref[0, :, cols[h]] = query_grad.T.astype(bf16)

    if previous:

        @pl.when(seq > 0)
        def _():
            earlier = [turned(pair_prev[0, d]).astype(bf16) for d in range(previous)]
            for h in range(heads):
                query_grad = nn(keys_turned, logit_grads[0, :, cols[h]])
                for d in range(previous):
                    query_grad = query_grad + nn(earlier[d], logit_grads[d + 1, :, cols[h]])
                qg_ref[0, :, cols[h]] = query_grad.T.astype(bf16)

    stores[1].start()
    key_sum, value_sum = pair_sums(0)
    pair_out[0, previous] = key_sum
    pair_out[1, previous] = value_sum
    wait_seq()
    gg_ref[...] = sum(gain_sum_slots[i] for i in range(n_seq))[:heads]
    stores[4].start()

    for distance in range(1, previous + 1):

        @pl.when(seq + distance < n_seq)
        def _():
            for index in range(2):
                grad_copy(index, distance).wait_recv()
                pair_out[index, previous] = (
                    pair_out[index, previous] + pair_in[index, distance - 1]
                )

    kg_ref[0] = pair_out[0, previous].astype(bf16)
    vg_ref[0] = pair_out[1, previous].astype(bf16)
    stores[2].start()
    stores[3].start()

    for distance in range(1, previous + 1):

        @pl.when(seq + distance < n_seq)
        def _():
            pair_copy(0, distance).wait_send()
            pair_copy(1, distance).wait_send()

        @pl.when(seq >= distance)
        def _():
            grad_copy(0, distance).wait_send()
            grad_copy(1, distance).wait_send()

    if n_seq > 1:

        @pl.when(seq < n_seq - 1)
        def _():
            for h in range(heads):
                state_copy(h).wait_send()

        @pl.when(seq > 0)
        def _():
            for h in range(heads):
                after_copy(h).wait_send()

    drain_squares()
    drain_slopes()
    drain_dp()
    drain_seq()
    for store in stores:
        store.wait()


def write_out(*refs):
    sources, targets, sems = refs[:5], refs[5:10], refs[10]
    copies = [
        pltpu.make_async_copy(source, target, sems.at[i])
        for i, (source, target) in enumerate(zip(sources, targets))
    ]
    for copy in copies:
        copy.start()
    for copy in copies:
        copy.wait()


def local(
    attention_queries,
    attention_keys,
    attention_values,
    key_window_length,
    norm_gain,
    spike_levels,
    lin_queries,
    lin_keys,
    decay_logs,
    cotangent,
):
    n_seq, n_dp, n_tensor = (lax.axis_size(axis) for axis in ("seq", "dp", "tensor"))
    rows = attention_queries.shape[1]
    heads = attention_queries.shape[2] // HEAD_SIZE
    previous = min((LONGEST_WINDOW + rows - 1) // rows, n_seq - 1)
    slots = max(previous, 1)
    state_type = bf16 if n_seq == 2 else f32
    size = HEAD_SIZE
    hbm = pl.BlockSpec(memory_space=pltpu.HBM)
    smem = pl.BlockSpec(memory_space=pltpu.SMEM)
    tiles = (heads, size, size)
    dma = pltpu.SemaphoreType.DMA
    outputs = (
        jax.ShapeDtypeStruct(attention_queries.shape, bf16),
        jax.ShapeDtypeStruct(attention_queries.shape, bf16),
        jax.ShapeDtypeStruct(attention_keys.shape, bf16),
        jax.ShapeDtypeStruct(attention_keys.shape, bf16),
        jax.ShapeDtypeStruct((heads, size), f32),
    )
    wide = pltpu.VMEM(attention_queries.shape, bf16)
    narrow = pltpu.VMEM(attention_keys.shape, bf16)
    scratch = [
        wide,
        wide,
        narrow,
        narrow,
        pltpu.VMEM((heads, size), f32),
        dma((5,)),
        wide,
        narrow,
        narrow,
        pltpu.VMEM((heads, size), f32),
        pltpu.VMEM((heads, size), jnp.int32),
        wide,
        wide,
        pltpu.VMEM((heads, 1, size), f32),
        wide,
        dma((9,)),
        pltpu.VMEM((2, slots, size, size), bf16),
        pltpu.VMEM((previous + 1,) + tiles, f32),
        pltpu.VMEM(tiles, f32),
        pltpu.VMEM(tiles, bf16),
        pltpu.VMEM(tiles, f32),
        pltpu.VMEM(tiles, f32),
        pltpu.VMEM(tiles, f32),
        pltpu.VMEM(tiles, f32),
        pltpu.VMEM(tiles, bf16),
        pltpu.VMEM(tiles, f32),
        pltpu.VMEM((size, heads * size), bf16),
        pltpu.VMEM((previous + 1, size, heads * size), bf16),
        pltpu.VMEM((previous + 1, size, heads * size), bf16),
        pltpu.VMEM((8, size), f32),
        pltpu.VMEM((8, size), f32),
        pltpu.VMEM((n_tensor, 8, size), f32),
        pltpu.VMEM((n_tensor, 8, size), f32),
        pltpu.VMEM(tiles, state_type),
        pltpu.VMEM(tiles, state_type),
        pltpu.VMEM(tiles, state_type),
        pltpu.VMEM(tiles, state_type),
        pltpu.VMEM((n_dp, 8, size), f32),
        pltpu.VMEM((n_seq, 8, size), f32),
        pltpu.VMEM((2, previous + 1, size, size), f32),
        pltpu.VMEM((2, slots, size, size), f32),
        dma((2, slots)),
        dma((2, slots)),
        dma((n_tensor,)),
        dma((n_tensor,)),
        dma((heads,)),
        dma((heads,)),
        dma((heads,)),
        dma((heads,)),
        dma((n_tensor,)),
        dma((n_tensor,)),
        dma((n_dp,)),
        dma((n_dp,)),
        dma((n_seq,)),
        dma((n_seq,)),
        dma((2, slots)),
        dma((2, slots)),
    ]
    results = pl.pallas_call(
        functools.partial(kernel, (n_seq, n_dp, n_tensor, previous, heads)),
        out_shape=outputs,
        in_specs=[hbm, hbm, hbm, smem] + [hbm] * 6,
        out_specs=(hbm,) * 5,
        scratch_shapes=scratch,
        compiler_params=pltpu.CompilerParams(
            collective_id=0, has_side_effects=True, vmem_limit_bytes=VMEM_LIMIT
        ),
        name="layer_pair",
    )(
        attention_queries,
        attention_keys,
        attention_values,
        key_window_length,
        norm_gain.reshape(heads, size),
        spike_levels.reshape(heads, size),
        lin_queries,
        lin_keys,
        decay_logs.reshape(heads, 1, rows),
        cotangent,
    )
    layer_output, query_grads, key_gradient, value_gradient, gain_grads = pl.pallas_call(
        write_out,
        out_shape=outputs,
        in_specs=[hbm] * 5,
        out_specs=(hbm,) * 5,
        scratch_shapes=[dma((5,))],
        compiler_params=pltpu.CompilerParams(vmem_limit_bytes=VMEM_LIMIT),
        name="write_out",
    )(*results)
    return (layer_output, query_grads, key_gradient, value_gradient, gain_grads.reshape(-1))


def solution(mesh):
    placed = (
        P("dp", "seq", "tensor"),
        P("dp", "seq", "tensor"),
        P("dp", "seq", "tensor"),
        P("tensor"),
        P("tensor"),
        P("tensor"),
        P("dp", "seq", "tensor"),
        P("dp", "seq", "tensor"),
        P("dp", "tensor", "seq"),
        P("dp", "seq", "tensor"),
    )
    return jax.shard_map(
        local,
        mesh=mesh,
        in_specs=placed,
        out_specs=(
            P("dp", "seq", "tensor"),
            P("dp", "seq", "tensor"),
            P("dp", "seq", "tensor"),
            P("dp", "seq", "tensor"),
            P("tensor"),
        ),
        check_vma=False,
    )
```

```python
import functools
import math

import jax
import jax.numpy as jnp
from jax import lax
from jax.experimental import pallas as pl
from jax.experimental.pallas import tpu as pltpu
from jax.sharding import PartitionSpec as P

HEAD_SIZE = 128
D = 3584
LONGEST_WINDOW = 512
VMEM_LIMIT = 63 * 1024 * 1024

MESH = pl.DeviceIdType.MESH
f32 = jnp.float32
bf16 = jnp.bfloat16
precise = lax.Precision.HIGHEST
epsilon = 1e-06


def nn(left, right):
    return lax.dot_general(left, right, (((1,), (0,)), ((), ())), preferred_element_type=f32)


def nt(left, right):
    return lax.dot_general(left, right, (((1,), (1,)), ((), ())), preferred_element_type=f32)


def turned(block):
    return block.astype(f32).T


def kernel(
    sizes,
    q_hbm,
    k_hbm,
    v_hbm,
    window_ref,
    gain_hbm,
    level_hbm,
    lq_hbm,
    lk_hbm,
    decay_hbm,
    ct_hbm,
    out_hbm,
    qg_hbm,
    kg_hbm,
    vg_hbm,
    gg_hbm,
    out_ref,
    qg_ref,
    kg_ref,
    vg_ref,
    gg_ref,
    store_sems,
    q_ref,
    k_ref,
    v_ref,
    gain_ref,
    level_ref,
    lq_ref,
    lk_ref,
    decay_ref,
    ct_ref,
    fetch_sems,
    pair_prev,
    probs,
    heads_out,
    decayed,
    ct_turned,
    gain_cols,
    level_cols,
    ratio_cols,
    bounded_buf,
    spikes_buf,
    work,
    out_grads,
    logit_grads,
    weights_buf,
    part_one,
    part_two,
    square_slots,
    slope_slots,
    state_out,
    state_in,
    after_out,
    after_in,
    gain_slots,
    gain_sum_slots,
    pair_out,
    pair_in,
    pair_send,
    pair_recv,
    square_send,
    square_recv,
    state_send,
    state_recv,
    after_send,
    after_recv,
    slope_send,
    slope_recv,
    dp_send,
    dp_recv,
    seq_send,
    seq_recv,
    grad_send,
    grad_recv,
):
    n_seq, n_dp, n_tensor, previous, heads = sizes
    seq, dp, ten = lax.axis_index("seq"), lax.axis_index("dp"), lax.axis_index("tensor")
    size = HEAD_SIZE
    scaling = 1.0 / math.sqrt(HEAD_SIZE)
    cols = [slice(h * size, (h + 1) * size) for h in range(heads)]

    barrier = pltpu.get_barrier_semaphore()
    for axis, me, count in (("seq", seq, n_seq), ("dp", dp, n_dp), ("tensor", ten, n_tensor)):
        for step in range(1, count):
            pl.semaphore_signal(
                barrier,
                inc=1,
                device_id={axis: lax.rem(me + step, count)},
                device_id_type=MESH,
            )
    fetches = [
        pltpu.make_async_copy(source, target, fetch_sems.at[i])
        for i, (source, target) in enumerate(
            (
                (k_hbm, k_ref),
                (q_hbm, q_ref),
                (v_hbm, v_ref),
                (decay_hbm, decay_ref),
                (gain_hbm, gain_ref),
                (level_hbm, level_ref),
                (lk_hbm, lk_ref),
                (lq_hbm, lq_ref),
                (ct_hbm, ct_ref),
            )
        )
    ]
    for fetch in fetches:
        fetch.start()
    stores = [
        pltpu.make_async_copy(source, target, store_sems.at[i])
        for i, (source, target) in enumerate(
            (
                (out_ref, out_hbm),
                (qg_ref, qg_hbm),
                (kg_ref, kg_hbm),
                (vg_ref, vg_hbm),
                (gg_ref, gg_hbm),
            )
        )
    ]
    pl.semaphore_wait(barrier, n_seq + n_dp + n_tensor - 3)

    def remote(src, dst, send, recv, axis, target):
        return pltpu.make_async_remote_copy(
            src_ref=src,
            dst_ref=dst,
            send_sem=send,
            recv_sem=recv,
            device_id={axis: target},
            device_id_type=MESH,
        )

    def exchange(slots, send, recv, axis, me, count):
        def start():
            for step in range(1, count):
                remote(
                    slots.at[me],
                    slots.at[me],
                    send.at[step - 1],
                    recv.at[me],
                    axis,
                    lax.rem(me + step, count),
                ).start()

        def wait():
            for step in range(1, count):
                sender = lax.rem(me + count - step, count)
                copy = remote(
                    slots.at[me], slots.at[sender], send.at[step - 1], recv.at[sender], axis, sender
                )
                copy.wait_recv()

        def drain():
            for step in range(1, count):
                remote(
                    slots.at[me],
                    slots.at[me],
                    send.at[step - 1],
                    recv.at[me],
                    axis,
                    lax.rem(me + step, count),
                ).wait_send()

        return start, wait, drain

    def pair_copy(index, distance):
        source = (k_hbm, v_hbm)[index].at[0]
        return remote(
            source,
            pair_prev.at[index, distance - 1],
            pair_send.at[index, distance - 1],
            pair_recv.at[index, distance - 1],
            "seq",
            lax.rem(seq + distance, n_seq),
        )

    def grad_copy(index, distance):
        return remote(
            pair_out.at[index, distance - 1],
            pair_in.at[index, distance - 1],
            grad_send.at[index, distance - 1],
            grad_recv.at[index, distance - 1],
            "seq",
            lax.rem(seq + n_seq - distance, n_seq),
        )

    for distance in range(1, previous + 1):

        @pl.when(seq + distance < n_seq)
        def _():
            pair_copy(0, distance).start()
            pair_copy(1, distance).start()

        @pl.when(seq < distance)
        def _():
            for index in range(2):
                pair_prev[index, distance - 1] = jnp.zeros((size, size), bf16)

    row_index = lax.broadcasted_iota(jnp.int32, (size, size), 0)
    column_index = lax.broadcasted_iota(jnp.int32, (size, size), 1)
    causal = row_index <= column_index
    window = window_ref[0]
    for fetch in fetches[:3]:
        fetch.wait()
    keys = k_ref[0]
    values = v_ref[0]
    keys_turned = turned(keys).astype(bf16)
    values_turned = turned(values).astype(bf16)

    for h in range(heads):
        scores = nt(keys, q_ref[0, :, cols[h]]) * scaling
        probs[0, h] = jnp.where(causal, scores, -jnp.inf)

    def attend(blocks):
        squares = jnp.zeros((size, size), f32)
        block_keys = [pair_prev[0, d] for d in range(blocks)]
        block_values = [turned(pair_prev[1, d]).astype(bf16) for d in range(blocks)]
        masks = []
        for d in range(blocks):
            seen = (d + 1) * size + column_index - row_index < window
            masks.append(seen & (seq > d) if n_seq > 2 else seen)
        for h in range(heads):
            scores = [probs[0, h]]
            for d in range(blocks):
                score = nt(block_keys[d], q_ref[0, :, cols[h]]) * scaling
                scores.append(jnp.where(masks[d], score, -jnp.inf))
            top = functools.reduce(
                jnp.maximum, [jnp.max(score, axis=0, keepdims=True) for score in scores]
            )
            exponents = [jnp.exp(score - top) for score in scores]
            total = sum(jnp.sum(exponent, axis=0, keepdims=True) for exponent in exponents)
            share = 1.0 / total
            result = None
            for d, exponent in enumerate(exponents):
                prob = exponent * share
                probs[d, h] = prob
                weights = prob.astype(bf16)
                weights_buf[d, :, cols[h]] = weights
                part = nn(values_turned if d == 0 else block_values[d - 1], weights)
                result = part if result is None else result + part
            result = result.astype(bf16).astype(f32)
            heads_out[h] = result
            squares = squares + result * result
        part_one[...] = jnp.broadcast_to(jnp.sum(squares, axis=0, keepdims=True), (8, size))

    @pl.when(seq == 0)
    def _():
        attend(0)

    if previous:

        @pl.when(seq > 0)
        def _():
            for distance in range(1, previous + 1):

                @pl.when(seq >= distance)
                def _():
                    pair_copy(0, distance).wait_recv()
                    pair_copy(1, distance).wait_recv()

            attend(previous)

    square_slots[ten] = part_one[...]
    start, wait_squares, drain_squares = exchange(
        square_slots, square_send, square_recv, "tensor", ten, n_tensor
    )
    start()

    for fetch in fetches[3:]:
        fetch.wait()
    logs = decay_ref[:, 0, :]
    upper = jnp.where(causal, 1.0, 0.0)
    cumulative = jnp.dot(logs, upper, precision=precise, preferred_element_type=f32)
    whole = jnp.dot(
        logs, jnp.ones((size, size), f32), precision=precise, preferred_element_type=f32
    )
    tail = jnp.exp(jnp.minimum(whole - cumulative, 0.0))
    grown = jnp.exp(cumulative)
    block_decay = jnp.exp(whole)
    for h in range(heads):
        level_rows = jnp.broadcast_to(level_ref[h : h + 1, :].astype(f32), (size, size))
        gain_rows = jnp.broadcast_to(gain_ref[h : h + 1, :], (size, size))
        level_cols[h] = level_rows.T
        gain_cols[h] = gain_rows.T
        ratio_cols[h] = (gain_rows / level_rows).T
        ct_turned[h] = turned(ct_ref[0, :, cols[h]])
        along = jnp.broadcast_to(cumulative[h : h + 1, :], (size, size))
        gaps = jnp.where(causal, along - along.T, -jnp.inf)
        product = nt(lk_ref[0, :, cols[h]], lq_ref[0, :, cols[h]])
        decayed[h] = (jnp.exp(gaps) * product).astype(bf16)

    wait_squares()
    square_sum = sum(square_slots[i] for i in range(n_tensor))[:1]
    inverse = lax.rsqrt(square_sum / D + epsilon)

    half = (heads + 1) // 2
    groups = [range(half), range(half, heads)]

    def state_copy(g):
        part = pl.ds(groups[g][0], len(groups[g]))
        return remote(
            state_out.at[part],
            state_in.at[part],
            state_send.at[g],
            state_recv.at[g],
            "seq",
            lax.rem(seq + 1, n_seq),
        )

    def after_copy(g):
        part = pl.ds(groups[g][0], len(groups[g]))
        return remote(
            after_out.at[part],
            after_in.at[part],
            after_send.at[g],
            after_recv.at[g],
            "seq",
            lax.rem(seq + n_seq - 1, n_seq),
        )

    for g, group in enumerate(groups):
        for h in group:
            normed = heads_out[h] * inverse
            heads_out[h] = normed
            bounded = jnp.tanh(normed * ratio_cols[h])
            bounded_buf[h] = bounded
            spikes = (level_cols[h] * bounded).astype(bf16)
            spikes_buf[h] = spikes
            fading = (spikes.astype(f32) * tail[h : h + 1]).astype(bf16)
            state_out[h] = nn(fading, lk_ref[0, :, cols[h]]).astype(state_out.dtype)
        if n_seq > 1:

            @pl.when(seq == 0)
            def _():
                state_copy(g).start()

    for h in range(heads):
        work[h] = nn(spikes_buf[h], decayed[h])

    if n_seq > 1:

        @pl.when(seq > 0)
        def _():
            for g, group in enumerate(groups):
                state_copy(g).wait_recv()
                if n_seq > 2:
                    for h in group:
                        state_out[h] = (
                            block_decay[h : h + 1] * state_in[h].astype(f32)
                            + state_out[h].astype(f32)
                        ).astype(state_out.dtype)

                    @pl.when(seq < n_seq - 1)
                    def _():
                        state_copy(g).start()

                for h in group:
                    carried = nt(state_in[h].astype(bf16), lq_ref[0, :, cols[h]])
                    work[h] = work[h] + grown[h : h + 1] * carried

    for g, group in enumerate(groups):
        for h in group:
            membrane = work[h]
            mean = jnp.sum(membrane * membrane, axis=0, keepdims=True) / size
            scale = lax.rsqrt(mean + epsilon)
            unit = membrane * scale
            incoming = ct_turned[h]
            inner = jnp.sum(incoming * unit, axis=0, keepdims=True) / size
            grad = scale * (incoming - unit * inner)
            ct_turned[h] = unit
            spikes_buf[h] = grad.astype(bf16)
            after_out[h] = nn((grad * grown[h : h + 1]).astype(bf16), lq_ref[0, :, cols[h]]).astype(
                after_out.dtype
            )
        if n_seq > 1:

            @pl.when(seq == n_seq - 1)
            def _():
                after_copy(g).start()

    for h in range(heads):
        work[h] = nt(spikes_buf[h], decayed[h])

    if n_seq > 1:

        @pl.when(seq < n_seq - 1)
        def _():
            for g, group in enumerate(groups):
                after_copy(g).wait_recv()
                if n_seq > 2:
                    for h in group:
                        after_out[h] = (
                            block_decay[h : h + 1] * after_in[h].astype(f32)
                            + after_out[h].astype(f32)
                        ).astype(after_out.dtype)

                    @pl.when(seq > 0)
                    def _():
                        after_copy(g).start()

                for h in group:
                    later = nt(after_in[h].astype(bf16), lk_ref[0, :, cols[h]])
                    work[h] = work[h] + tail[h : h + 1] * later

    slope_part = jnp.zeros((size, size), f32)
    for h in range(heads):
        bounded = bounded_buf[h]
        level_grad = work[h] * (1.0 - bounded * bounded)
        with_normed = level_grad * heads_out[h]
        work[h] = level_grad
        bounded_buf[h] = with_normed
        slope_part = slope_part + with_normed * gain_cols[h]
    part_two[...] = jnp.broadcast_to(jnp.sum(slope_part, axis=0, keepdims=True), (8, size))
    slope_slots[ten] = part_two[...]
    start, wait_slopes, drain_slopes = exchange(
        slope_slots, slope_send, slope_recv, "tensor", ten, n_tensor
    )
    start()

    rows = [jnp.sum(bounded_buf[h].T, axis=0, keepdims=True) for h in range(heads)]
    rows.append(jnp.zeros((8 - heads, size), f32))
    gain_slots[dp] = jnp.concatenate(rows, axis=0)
    start, wait_dp, drain_dp = exchange(gain_slots, dp_send, dp_recv, "dp", dp, n_dp)
    start()

    for h in range(heads):
        out_ref[0, :, cols[h]] = ct_turned[h].T.astype(bf16)
    stores[0].start()

    wait_slopes()
    slope = sum(slope_slots[i] for i in range(n_tensor))[:1] / D
    for h in range(heads):
        normed_grad = work[h] * gain_cols[h]
        out_grads[:, cols[h]] = (inverse * (normed_grad - heads_out[h] * slope)).astype(bf16)

    def back(blocks):
        block_values = [values] + [pair_prev[1, d] for d in range(blocks)]
        for h in range(heads):
            prob_grads = [nn(block, out_grads[:, cols[h]]) for block in block_values]
            delta = sum(
                jnp.sum(probs[d, h] * prob_grad, axis=0, keepdims=True)
                for d, prob_grad in enumerate(prob_grads)
            )
            for d, prob_grad in enumerate(prob_grads):
                logit_grad = probs[d, h] * (prob_grad - delta) * scaling
                logit_grads[d, :, cols[h]] = logit_grad.astype(bf16)

    def pair_sums(d):
        key_sum = sum(nn(logit_grads[d, :, cols[h]], q_ref[0, :, cols[h]]) for h in range(heads))
        value_sum = nt(weights_buf[d], out_grads[...])
        return key_sum, value_sum

    @pl.when(seq == 0)
    def _():
        back(0)

    if previous:

        @pl.when(seq > 0)
        def _():
            back(previous)
            for distance in range(1, previous + 1):
                key_sum, value_sum = pair_sums(distance)
                pair_out[0, distance - 1] = key_sum
                pair_out[1, distance - 1] = value_sum

                @pl.when(seq >= distance)
                def _():
                    grad_copy(0, distance).start()
                    grad_copy(1, distance).start()

    wait_dp()
    gain_sum_slots[seq] = sum(gain_slots[i] for i in range(n_dp))
    start, wait_seq, drain_seq = exchange(gain_sum_slots, seq_send, seq_recv, "seq", seq, n_seq)
    start()

    @pl.when(seq == 0)
    def _():
        for h in range(heads):
            query_grad = nn(keys_turned, logit_grads[0, :, cols[h]])
            qg_ref[0, :, cols[h]] = query_grad.T.astype(bf16)

    if previous:

        @pl.when(seq > 0)
        def _():
            earlier = [turned(pair_prev[0, d]).astype(bf16) for d in range(previous)]
            for h in range(heads):
                query_grad = nn(keys_turned, logit_grads[0, :, cols[h]])
                for d in range(previous):
                    query_grad = query_grad + nn(earlier[d], logit_grads[d + 1, :, cols[h]])
                qg_ref[0, :, cols[h]] = query_grad.T.astype(bf16)

    stores[1].start()
    key_sum, value_sum = pair_sums(0)
    pair_out[0, previous] = key_sum
    pair_out[1, previous] = value_sum
    wait_seq()
    gg_ref[...] = sum(gain_sum_slots[i] for i in range(n_seq))[:heads]
    stores[4].start()

    for distance in range(1, previous + 1):

        @pl.when(seq + distance < n_seq)
        def _():
            for index in range(2):
                grad_copy(index, distance).wait_recv()
                pair_out[index, previous] = (
                    pair_out[index, previous] + pair_in[index, distance - 1]
                )

    kg_ref[0] = pair_out[0, previous].astype(bf16)
    vg_ref[0] = pair_out[1, previous].astype(bf16)
    stores[2].start()
    stores[3].start()

    for distance in range(1, previous + 1):

        @pl.when(seq + distance < n_seq)
        def _():
            pair_copy(0, distance).wait_send()
            pair_copy(1, distance).wait_send()

        @pl.when(seq >= distance)
        def _():
            grad_copy(0, distance).wait_send()
            grad_copy(1, distance).wait_send()

    if n_seq > 1:

        @pl.when(seq < n_seq - 1)
        def _():
            for g in range(2):
                state_copy(g).wait_send()

        @pl.when(seq > 0)
        def _():
            for g in range(2):
                after_copy(g).wait_send()

    drain_squares()
    drain_slopes()
    drain_dp()
    drain_seq()
    for store in stores:
        store.wait()


def write_out(*refs):
    sources, targets, held, sems = refs[:5], refs[5:10], refs[10:15], refs[15]
    reads = [pltpu.make_async_copy(sources[i], held[i], sems.at[0, i]) for i in range(5)]
    writes = [pltpu.make_async_copy(held[i], targets[i], sems.at[1, i]) for i in range(5)]
    for read in reads:
        read.start()
    for read, write in zip(reads, writes):
        read.wait()
        write.start()
    for write in writes:
        write.wait()


def local(
    attention_queries,
    attention_keys,
    attention_values,
    key_window_length,
    norm_gain,
    spike_levels,
    lin_queries,
    lin_keys,
    decay_logs,
    cotangent,
):
    n_seq, n_dp, n_tensor = (lax.axis_size(axis) for axis in ("seq", "dp", "tensor"))
    rows = attention_queries.shape[1]
    heads = attention_queries.shape[2] // HEAD_SIZE
    previous = min((LONGEST_WINDOW + rows - 1) // rows, n_seq - 1)
    slots = max(previous, 1)
    state_type = bf16 if n_seq == 2 else f32
    size = HEAD_SIZE
    hbm = pl.BlockSpec(memory_space=pltpu.HBM)
    smem = pl.BlockSpec(memory_space=pltpu.SMEM)
    tiles = (heads, size, size)
    dma = pltpu.SemaphoreType.DMA
    outputs = (
        jax.ShapeDtypeStruct(attention_queries.shape, bf16),
        jax.ShapeDtypeStruct(attention_queries.shape, bf16),
        jax.ShapeDtypeStruct(attention_keys.shape, bf16),
        jax.ShapeDtypeStruct(attention_keys.shape, bf16),
        jax.ShapeDtypeStruct((heads, size), f32),
    )
    wide = pltpu.VMEM(attention_queries.shape, bf16)
    narrow = pltpu.VMEM(attention_keys.shape, bf16)
    scratch = [
        wide,
        wide,
        narrow,
        narrow,
        pltpu.VMEM((heads, size), f32),
        dma((5,)),
        wide,
        narrow,
        narrow,
        pltpu.VMEM((heads, size), f32),
        pltpu.VMEM((heads, size), jnp.int32),
        wide,
        wide,
        pltpu.VMEM((heads, 1, size), f32),
        wide,
        dma((9,)),
        pltpu.VMEM((2, slots, size, size), bf16),
        pltpu.VMEM((previous + 1,) + tiles, f32),
        pltpu.VMEM(tiles, f32),
        pltpu.VMEM(tiles, bf16),
        pltpu.VMEM(tiles, f32),
        pltpu.VMEM(tiles, f32),
        pltpu.VMEM(tiles, f32),
        pltpu.VMEM(tiles, f32),
        pltpu.VMEM(tiles, f32),
        pltpu.VMEM(tiles, bf16),
        pltpu.VMEM(tiles, f32),
        pltpu.VMEM((size, heads * size), bf16),
        pltpu.VMEM((previous + 1, size, heads * size), bf16),
        pltpu.VMEM((previous + 1, size, heads * size), bf16),
        pltpu.VMEM((8, size), f32),
        pltpu.VMEM((8, size), f32),
        pltpu.VMEM((n_tensor, 8, size), f32),
        pltpu.VMEM((n_tensor, 8, size), f32),
        pltpu.VMEM(tiles, state_type),
        pltpu.VMEM(tiles, state_type),
        pltpu.VMEM(tiles, state_type),
        pltpu.VMEM(tiles, state_type),
        pltpu.VMEM((n_dp, 8, size), f32),
        pltpu.VMEM((n_seq, 8, size), f32),
        pltpu.VMEM((2, previous + 1, size, size), f32),
        pltpu.VMEM((2, slots, size, size), f32),
        dma((2, slots)),
        dma((2, slots)),
        dma((n_tensor,)),
        dma((n_tensor,)),
        dma((2,)),
        dma((2,)),
        dma((2,)),
        dma((2,)),
        dma((n_tensor,)),
        dma((n_tensor,)),
        dma((n_dp,)),
        dma((n_dp,)),
        dma((n_seq,)),
        dma((n_seq,)),
        dma((2, slots)),
        dma((2, slots)),
    ]
    results = pl.pallas_call(
        functools.partial(kernel, (n_seq, n_dp, n_tensor, previous, heads)),
        out_shape=outputs,
        in_specs=[hbm, hbm, hbm, smem] + [hbm] * 6,
        out_specs=(hbm,) * 5,
        scratch_shapes=scratch,
        compiler_params=pltpu.CompilerParams(
            collective_id=0, has_side_effects=True, vmem_limit_bytes=VMEM_LIMIT
        ),
        name="layer_pair",
    )(
        attention_queries,
        attention_keys,
        attention_values,
        key_window_length,
        norm_gain.reshape(heads, size),
        spike_levels.reshape(heads, size),
        lin_queries,
        lin_keys,
        decay_logs.reshape(heads, 1, rows),
        cotangent,
    )
    layer_output, query_grads, key_gradient, value_gradient, gain_grads = pl.pallas_call(
        write_out,
        out_shape=outputs,
        in_specs=[hbm] * 5,
        out_specs=(hbm,) * 5,
        scratch_shapes=[pltpu.VMEM(out.shape, out.dtype) for out in outputs] + [dma((2, 5))],
        compiler_params=pltpu.CompilerParams(vmem_limit_bytes=VMEM_LIMIT),
        name="write_out",
    )(*results)
    return (layer_output, query_grads, key_gradient, value_gradient, gain_grads.reshape(-1))


def solution(mesh):
    placed = (
        P("dp", "seq", "tensor"),
        P("dp", "seq", "tensor"),
        P("dp", "seq", "tensor"),
        P("tensor"),
        P("tensor"),
        P("tensor"),
        P("dp", "seq", "tensor"),
        P("dp", "seq", "tensor"),
        P("dp", "tensor", "seq"),
        P("dp", "seq", "tensor"),
    )
    return jax.shard_map(
        local,
        mesh=mesh,
        in_specs=placed,
        out_specs=(
            P("dp", "seq", "tensor"),
            P("dp", "seq", "tensor"),
            P("dp", "seq", "tensor"),
            P("dp", "seq", "tensor"),
            P("tensor"),
        ),
        check_vma=False,
    )
```

```python
import functools
import math

import jax
import jax.numpy as jnp
from jax import lax
from jax.experimental import pallas as pl
from jax.experimental.pallas import tpu as pltpu
from jax.sharding import PartitionSpec as P

HEAD_SIZE = 128
D = 3584
LONGEST_WINDOW = 512
VMEM_LIMIT = 62 * 1024 * 1024
WRITE_LIMIT = 4 * 1024 * 1024

MESH = pl.DeviceIdType.MESH
f32 = jnp.float32
bf16 = jnp.bfloat16
precise = lax.Precision.HIGHEST
epsilon = 1e-06


def nn(left, right):
    return lax.dot_general(left, right, (((1,), (0,)), ((), ())), preferred_element_type=f32)


def nt(left, right):
    return lax.dot_general(left, right, (((1,), (1,)), ((), ())), preferred_element_type=f32)


def turned(block):
    return block.astype(f32).T


def kernel(
    sizes,
    q_hbm,
    k_hbm,
    v_hbm,
    window_ref,
    gain_hbm,
    level_hbm,
    lq_hbm,
    lk_hbm,
    decay_hbm,
    ct_hbm,
    out_ref,
    qg_ref,
    kg_ref,
    vg_ref,
    gg_ref,
    q_ref,
    k_ref,
    v_ref,
    gain_ref,
    level_ref,
    lq_ref,
    lk_ref,
    decay_ref,
    ct_ref,
    fetch_sems,
    pair_prev,
    probs,
    heads_out,
    decayed,
    ct_turned,
    gain_cols,
    level_cols,
    ratio_cols,
    bounded_buf,
    spikes_buf,
    work,
    out_grads,
    logit_grads,
    weights_buf,
    part_one,
    part_two,
    square_slots,
    slope_slots,
    state_out,
    state_in,
    after_out,
    after_in,
    gain_slots,
    gain_sum_slots,
    pair_out,
    pair_in,
    pair_send,
    pair_recv,
    square_send,
    square_recv,
    state_send,
    state_recv,
    after_send,
    after_recv,
    slope_send,
    slope_recv,
    dp_send,
    dp_recv,
    seq_send,
    seq_recv,
    grad_send,
    grad_recv,
):
    n_seq, n_dp, n_tensor, previous, heads = sizes
    seq, dp, ten = lax.axis_index("seq"), lax.axis_index("dp"), lax.axis_index("tensor")
    size = HEAD_SIZE
    scaling = 1.0 / math.sqrt(HEAD_SIZE)
    cols = [slice(h * size, (h + 1) * size) for h in range(heads)]

    barrier = pltpu.get_barrier_semaphore()
    for axis, me, count in (("seq", seq, n_seq), ("dp", dp, n_dp), ("tensor", ten, n_tensor)):
        for step in range(1, count):
            pl.semaphore_signal(
                barrier,
                inc=1,
                device_id={axis: lax.rem(me + step, count)},
                device_id_type=MESH,
            )
    fetches = [
        pltpu.make_async_copy(source, target, fetch_sems.at[i])
        for i, (source, target) in enumerate(
            (
                (k_hbm, k_ref),
                (q_hbm, q_ref),
                (v_hbm, v_ref),
                (decay_hbm, decay_ref),
                (gain_hbm, gain_ref),
                (level_hbm, level_ref),
                (lk_hbm, lk_ref),
                (lq_hbm, lq_ref),
                (ct_hbm, ct_ref),
            )
        )
    ]
    for fetch in fetches:
        fetch.start()
    pl.semaphore_wait(barrier, n_seq + n_dp + n_tensor - 3)

    def remote(src, dst, send, recv, axis, target):
        return pltpu.make_async_remote_copy(
            src_ref=src,
            dst_ref=dst,
            send_sem=send,
            recv_sem=recv,
            device_id={axis: target},
            device_id_type=MESH,
        )

    def exchange(slots, send, recv, axis, me, count):
        def start():
            for step in range(1, count):
                remote(
                    slots.at[me],
                    slots.at[me],
                    send.at[step - 1],
                    recv.at[me],
                    axis,
                    lax.rem(me + step, count),
                ).start()

        def wait():
            for step in range(1, count):
                sender = lax.rem(me + count - step, count)
                copy = remote(
                    slots.at[me], slots.at[sender], send.at[step - 1], recv.at[sender], axis, sender
                )
                copy.wait_recv()

        def drain():
            for step in range(1, count):
                remote(
                    slots.at[me],
                    slots.at[me],
                    send.at[step - 1],
                    recv.at[me],
                    axis,
                    lax.rem(me + step, count),
                ).wait_send()

        return start, wait, drain

    def pair_copy(index, distance):
        source = (k_hbm, v_hbm)[index].at[0]
        return remote(
            source,
            pair_prev.at[index, distance - 1],
            pair_send.at[index, distance - 1],
            pair_recv.at[index, distance - 1],
            "seq",
            lax.rem(seq + distance, n_seq),
        )

    def grad_copy(index, distance):
        return remote(
            pair_out.at[index, distance - 1],
            pair_in.at[index, distance - 1],
            grad_send.at[index, distance - 1],
            grad_recv.at[index, distance - 1],
            "seq",
            lax.rem(seq + n_seq - distance, n_seq),
        )

    for distance in range(1, previous + 1):

        @pl.when(seq + distance < n_seq)
        def _():
            pair_copy(0, distance).start()
            pair_copy(1, distance).start()

        @pl.when(seq < distance)
        def _():
            for index in range(2):
                pair_prev[index, distance - 1] = jnp.zeros((size, size), bf16)

    row_index = lax.broadcasted_iota(jnp.int32, (size, size), 0)
    column_index = lax.broadcasted_iota(jnp.int32, (size, size), 1)
    causal = row_index <= column_index
    window = window_ref[0]
    for fetch in fetches[:3]:
        fetch.wait()
    keys = k_ref[0]
    values = v_ref[0]
    keys_turned = turned(keys).astype(bf16)
    values_turned = turned(values).astype(bf16)

    for h in range(heads):
        scores = nt(keys, q_ref[0, :, cols[h]]) * scaling
        probs[0, h] = jnp.where(causal, scores, -jnp.inf)

    def attend(blocks):
        squares = jnp.zeros((size, size), f32)
        block_keys = [pair_prev[0, d] for d in range(blocks)]
        block_values = [turned(pair_prev[1, d]).astype(bf16) for d in range(blocks)]
        masks = []
        for d in range(blocks):
            seen = (d + 1) * size + column_index - row_index < window
            masks.append(seen & (seq > d) if n_seq > 2 else seen)
        for h in range(heads):
            scores = [probs[0, h]]
            for d in range(blocks):
                score = nt(block_keys[d], q_ref[0, :, cols[h]]) * scaling
                scores.append(jnp.where(masks[d], score, -jnp.inf))
            top = functools.reduce(
                jnp.maximum, [jnp.max(score, axis=0, keepdims=True) for score in scores]
            )
            exponents = [jnp.exp(score - top) for score in scores]
            total = sum(jnp.sum(exponent, axis=0, keepdims=True) for exponent in exponents)
            share = 1.0 / total
            result = None
            for d, exponent in enumerate(exponents):
                prob = exponent * share
                probs[d, h] = prob
                weights = prob.astype(bf16)
                weights_buf[d, :, cols[h]] = weights
                part = nn(values_turned if d == 0 else block_values[d - 1], weights)
                result = part if result is None else result + part
            result = result.astype(bf16).astype(f32)
            heads_out[h] = result
            squares = squares + result * result
        part_one[...] = jnp.broadcast_to(jnp.sum(squares, axis=0, keepdims=True), (8, size))

    @pl.when(seq == 0)
    def _():
        attend(0)

    if previous:

        @pl.when(seq > 0)
        def _():
            for distance in range(1, previous + 1):

                @pl.when(seq >= distance)
                def _():
                    pair_copy(0, distance).wait_recv()
                    pair_copy(1, distance).wait_recv()

            attend(previous)

    square_slots[ten] = part_one[...]
    start, wait_squares, drain_squares = exchange(
        square_slots, square_send, square_recv, "tensor", ten, n_tensor
    )
    start()

    for fetch in fetches[3:]:
        fetch.wait()
    logs = decay_ref[:, 0, :]
    upper = jnp.where(causal, 1.0, 0.0)
    cumulative = jnp.dot(logs, upper, precision=precise, preferred_element_type=f32)
    whole = jnp.dot(
        logs, jnp.ones((size, size), f32), precision=precise, preferred_element_type=f32
    )
    tail = jnp.exp(jnp.minimum(whole - cumulative, 0.0))
    grown = jnp.exp(cumulative)
    block_decay = jnp.exp(whole)
    for h in range(heads):
        level_rows = jnp.broadcast_to(level_ref[h : h + 1, :].astype(f32), (size, size))
        gain_rows = jnp.broadcast_to(gain_ref[h : h + 1, :], (size, size))
        level_cols[h] = level_rows.T
        gain_cols[h] = gain_rows.T
        ratio_cols[h] = (gain_rows / level_rows).T
        ct_turned[h] = turned(ct_ref[0, :, cols[h]])
        along = jnp.broadcast_to(cumulative[h : h + 1, :], (size, size))
        gaps = jnp.where(causal, along - along.T, -jnp.inf)
        product = nt(lk_ref[0, :, cols[h]], lq_ref[0, :, cols[h]])
        decayed[h] = (jnp.exp(gaps) * product).astype(bf16)

    wait_squares()
    square_sum = sum(square_slots[i] for i in range(n_tensor))[:1]
    inverse = lax.rsqrt(square_sum / D + epsilon)

    half = (heads + 1) // 2
    groups = [range(half), range(half, heads)]

    def state_copy(g):
        part = pl.ds(groups[g][0], len(groups[g]))
        return remote(
            state_out.at[part],
            state_in.at[part],
            state_send.at[g],
            state_recv.at[g],
            "seq",
            lax.rem(seq + 1, n_seq),
        )

    def after_copy(g):
        part = pl.ds(groups[g][0], len(groups[g]))
        return remote(
            after_out.at[part],
            after_in.at[part],
            after_send.at[g],
            after_recv.at[g],
            "seq",
            lax.rem(seq + n_seq - 1, n_seq),
        )

    for g, group in enumerate(groups):
        for h in group:
            normed = heads_out[h] * inverse
            heads_out[h] = normed
            bounded = jnp.tanh(normed * ratio_cols[h])
            bounded_buf[h] = bounded
            spikes = (level_cols[h] * bounded).astype(bf16)
            spikes_buf[h] = spikes
            fading = (spikes.astype(f32) * tail[h : h + 1]).astype(bf16)
            state_out[h] = nn(fading, lk_ref[0, :, cols[h]]).astype(state_out.dtype)
        if n_seq > 1:

            @pl.when(seq == 0)
            def _():
                state_copy(g).start()

    for h in range(heads):
        work[h] = nn(spikes_buf[h], decayed[h])

    if n_seq > 1:

        @pl.when(seq > 0)
        def _():
            for g, group in enumerate(groups):
                state_copy(g).wait_recv()
                if n_seq > 2:
                    for h in group:
                        state_out[h] = (
                            block_decay[h : h + 1] * state_in[h].astype(f32)
                            + state_out[h].astype(f32)
                        ).astype(state_out.dtype)

                    @pl.when(seq < n_seq - 1)
                    def _():
                        state_copy(g).start()

                for h in group:
                    carried = nt(state_in[h].astype(bf16), lq_ref[0, :, cols[h]])
                    work[h] = work[h] + grown[h : h + 1] * carried

    for g, group in enumerate(groups):
        for h in group:
            membrane = work[h]
            mean = jnp.sum(membrane * membrane, axis=0, keepdims=True) / size
            scale = lax.rsqrt(mean + epsilon)
            unit = membrane * scale
            incoming = ct_turned[h]
            inner = jnp.sum(incoming * unit, axis=0, keepdims=True) / size
            grad = scale * (incoming - unit * inner)
            ct_turned[h] = unit
            spikes_buf[h] = grad.astype(bf16)
            after_out[h] = nn((grad * grown[h : h + 1]).astype(bf16), lq_ref[0, :, cols[h]]).astype(
                after_out.dtype
            )
        if n_seq > 1:

            @pl.when(seq == n_seq - 1)
            def _():
                after_copy(g).start()

    for h in range(heads):
        work[h] = nt(spikes_buf[h], decayed[h])

    if n_seq > 1:

        @pl.when(seq < n_seq - 1)
        def _():
            for g, group in enumerate(groups):
                after_copy(g).wait_recv()
                if n_seq > 2:
                    for h in group:
                        after_out[h] = (
                            block_decay[h : h + 1] * after_in[h].astype(f32)
                            + after_out[h].astype(f32)
                        ).astype(after_out.dtype)

                    @pl.when(seq > 0)
                    def _():
                        after_copy(g).start()

                for h in group:
                    later = nt(after_in[h].astype(bf16), lk_ref[0, :, cols[h]])
                    work[h] = work[h] + tail[h : h + 1] * later

    slope_part = jnp.zeros((size, size), f32)
    for h in range(heads):
        bounded = bounded_buf[h]
        level_grad = work[h] * (1.0 - bounded * bounded)
        with_normed = level_grad * heads_out[h]
        work[h] = level_grad
        bounded_buf[h] = with_normed
        slope_part = slope_part + with_normed * gain_cols[h]
    part_two[...] = jnp.broadcast_to(jnp.sum(slope_part, axis=0, keepdims=True), (8, size))
    slope_slots[ten] = part_two[...]
    start, wait_slopes, drain_slopes = exchange(
        slope_slots, slope_send, slope_recv, "tensor", ten, n_tensor
    )
    start()

    rows = [jnp.sum(bounded_buf[h].T, axis=0, keepdims=True) for h in range(heads)]
    rows.append(jnp.zeros((8 - heads, size), f32))
    gain_slots[dp] = jnp.concatenate(rows, axis=0)
    start, wait_dp, drain_dp = exchange(gain_slots, dp_send, dp_recv, "dp", dp, n_dp)
    start()

    for h in range(heads):
        out_ref[0, :, cols[h]] = ct_turned[h].T.astype(bf16)

    wait_slopes()
    slope = sum(slope_slots[i] for i in range(n_tensor))[:1] / D
    for h in range(heads):
        normed_grad = work[h] * gain_cols[h]
        out_grads[:, cols[h]] = (inverse * (normed_grad - heads_out[h] * slope)).astype(bf16)

    def back(blocks):
        block_values = [values] + [pair_prev[1, d] for d in range(blocks)]
        for h in range(heads):
            prob_grads = [nn(block, out_grads[:, cols[h]]) for block in block_values]
            delta = sum(
                jnp.sum(probs[d, h] * prob_grad, axis=0, keepdims=True)
                for d, prob_grad in enumerate(prob_grads)
            )
            for d, prob_grad in enumerate(prob_grads):
                logit_grad = probs[d, h] * (prob_grad - delta) * scaling
                logit_grads[d, :, cols[h]] = logit_grad.astype(bf16)

    def key_sum(d):
        return sum(nn(logit_grads[d, :, cols[h]], q_ref[0, :, cols[h]]) for h in range(heads))

    def value_sum(d):
        return nt(weights_buf[d], out_grads[...])

    @pl.when(seq == 0)
    def _():
        back(0)

    if previous:

        @pl.when(seq > 0)
        def _():
            for distance in range(1, previous + 1):
                pair_out[1, distance - 1] = value_sum(distance)

                @pl.when(seq >= distance)
                def _():
                    grad_copy(1, distance).start()

            back(previous)
            for distance in range(1, previous + 1):
                pair_out[0, distance - 1] = key_sum(distance)

                @pl.when(seq >= distance)
                def _():
                    grad_copy(0, distance).start()

    wait_dp()
    gain_sum_slots[seq] = sum(gain_slots[i] for i in range(n_dp))
    start, wait_seq, drain_seq = exchange(gain_sum_slots, seq_send, seq_recv, "seq", seq, n_seq)
    start()

    @pl.when(seq == 0)
    def _():
        for h in range(heads):
            query_grad = nn(keys_turned, logit_grads[0, :, cols[h]])
            qg_ref[0, :, cols[h]] = query_grad.T.astype(bf16)

    if previous:

        @pl.when(seq > 0)
        def _():
            earlier = [turned(pair_prev[0, d]).astype(bf16) for d in range(previous)]
            for h in range(heads):
                query_grad = nn(keys_turned, logit_grads[0, :, cols[h]])
                for d in range(previous):
                    query_grad = query_grad + nn(earlier[d], logit_grads[d + 1, :, cols[h]])
                qg_ref[0, :, cols[h]] = query_grad.T.astype(bf16)

    pair_out[0, previous] = key_sum(0)
    pair_out[1, previous] = value_sum(0)
    wait_seq()
    gg_ref[...] = sum(gain_sum_slots[i] for i in range(n_seq))[:heads]

    for distance in range(1, previous + 1):

        @pl.when(seq + distance < n_seq)
        def _():
            for index in range(2):
                grad_copy(index, distance).wait_recv()
                pair_out[index, previous] = (
                    pair_out[index, previous] + pair_in[index, distance - 1]
                )

    kg_ref[0] = pair_out[0, previous].astype(bf16)
    vg_ref[0] = pair_out[1, previous].astype(bf16)

    for distance in range(1, previous + 1):

        @pl.when(seq + distance < n_seq)
        def _():
            pair_copy(0, distance).wait_send()
            pair_copy(1, distance).wait_send()

        @pl.when(seq >= distance)
        def _():
            grad_copy(0, distance).wait_send()
            grad_copy(1, distance).wait_send()

    if n_seq > 1:

        @pl.when(seq < n_seq - 1)
        def _():
            for g in range(2):
                state_copy(g).wait_send()

        @pl.when(seq > 0)
        def _():
            for g in range(2):
                after_copy(g).wait_send()

    drain_squares()
    drain_slopes()
    drain_dp()
    drain_seq()


def write_out(*refs):
    sources, targets, sems = refs[:5], refs[5:10], refs[10]
    writes = [pltpu.make_async_copy(sources[i], targets[i], sems.at[i]) for i in range(5)]
    for write in writes:
        write.start()
    for write in writes:
        write.wait()


def local(
    attention_queries,
    attention_keys,
    attention_values,
    key_window_length,
    norm_gain,
    spike_levels,
    lin_queries,
    lin_keys,
    decay_logs,
    cotangent,
):
    n_seq, n_dp, n_tensor = (lax.axis_size(axis) for axis in ("seq", "dp", "tensor"))
    rows = attention_queries.shape[1]
    heads = attention_queries.shape[2] // HEAD_SIZE
    previous = min((LONGEST_WINDOW + rows - 1) // rows, n_seq - 1)
    slots = max(previous, 1)
    state_type = bf16 if n_seq == 2 else f32
    size = HEAD_SIZE
    hbm = pl.BlockSpec(memory_space=pltpu.HBM)
    vmem = pl.BlockSpec(memory_space=pltpu.VMEM)
    smem = pl.BlockSpec(memory_space=pltpu.SMEM)
    tiles = (heads, size, size)
    dma = pltpu.SemaphoreType.DMA
    outputs = (
        jax.ShapeDtypeStruct(attention_queries.shape, bf16),
        jax.ShapeDtypeStruct(attention_queries.shape, bf16),
        jax.ShapeDtypeStruct(attention_keys.shape, bf16),
        jax.ShapeDtypeStruct(attention_keys.shape, bf16),
        jax.ShapeDtypeStruct((heads, size), f32),
    )
    wide = pltpu.VMEM(attention_queries.shape, bf16)
    narrow = pltpu.VMEM(attention_keys.shape, bf16)
    scratch = [
        wide,
        narrow,
        narrow,
        pltpu.VMEM((heads, size), f32),
        pltpu.VMEM((heads, size), jnp.int32),
        wide,
        wide,
        pltpu.VMEM((heads, 1, size), f32),
        wide,
        dma((9,)),
        pltpu.VMEM((2, slots, size, size), bf16),
        pltpu.VMEM((previous + 1,) + tiles, f32),
        pltpu.VMEM(tiles, f32),
        pltpu.VMEM(tiles, bf16),
        pltpu.VMEM(tiles, f32),
        pltpu.VMEM(tiles, f32),
        pltpu.VMEM(tiles, f32),
        pltpu.VMEM(tiles, f32),
        pltpu.VMEM(tiles, f32),
        pltpu.VMEM(tiles, bf16),
        pltpu.VMEM(tiles, f32),
        pltpu.VMEM((size, heads * size), bf16),
        pltpu.VMEM((previous + 1, size, heads * size), bf16),
        pltpu.VMEM((previous + 1, size, heads * size), bf16),
        pltpu.VMEM((8, size), f32),
        pltpu.VMEM((8, size), f32),
        pltpu.VMEM((n_tensor, 8, size), f32),
        pltpu.VMEM((n_tensor, 8, size), f32),
        pltpu.VMEM(tiles, state_type),
        pltpu.VMEM(tiles, state_type),
        pltpu.VMEM(tiles, state_type),
        pltpu.VMEM(tiles, state_type),
        pltpu.VMEM((n_dp, 8, size), f32),
        pltpu.VMEM((n_seq, 8, size), f32),
        pltpu.VMEM((2, previous + 1, size, size), f32),
        pltpu.VMEM((2, slots, size, size), f32),
        dma((2, slots)),
        dma((2, slots)),
        dma((n_tensor,)),
        dma((n_tensor,)),
        dma((2,)),
        dma((2,)),
        dma((2,)),
        dma((2,)),
        dma((n_tensor,)),
        dma((n_tensor,)),
        dma((n_dp,)),
        dma((n_dp,)),
        dma((n_seq,)),
        dma((n_seq,)),
        dma((2, slots)),
        dma((2, slots)),
    ]
    results = pl.pallas_call(
        functools.partial(kernel, (n_seq, n_dp, n_tensor, previous, heads)),
        out_shape=tuple(pltpu.VMEM(out.shape, out.dtype) for out in outputs),
        in_specs=[hbm, hbm, hbm, smem] + [hbm] * 6,
        out_specs=(vmem,) * 5,
        scratch_shapes=scratch,
        compiler_params=pltpu.CompilerParams(
            collective_id=0, has_side_effects=True, vmem_limit_bytes=VMEM_LIMIT
        ),
        name="layer_pair",
    )(
        attention_queries,
        attention_keys,
        attention_values,
        key_window_length,
        norm_gain.reshape(heads, size),
        spike_levels.reshape(heads, size),
        lin_queries,
        lin_keys,
        decay_logs.reshape(heads, 1, rows),
        cotangent,
    )
    layer_output, query_grads, key_gradient, value_gradient, gain_grads = pl.pallas_call(
        write_out,
        out_shape=outputs,
        in_specs=[vmem] * 5,
        out_specs=(hbm,) * 5,
        scratch_shapes=[dma((5,))],
        compiler_params=pltpu.CompilerParams(vmem_limit_bytes=WRITE_LIMIT),
        name="write_out",
    )(*results)
    return (layer_output, query_grads, key_gradient, value_gradient, gain_grads.reshape(-1))


def solution(mesh):
    placed = (
        P("dp", "seq", "tensor"),
        P("dp", "seq", "tensor"),
        P("dp", "seq", "tensor"),
        P("tensor"),
        P("tensor"),
        P("tensor"),
        P("dp", "seq", "tensor"),
        P("dp", "seq", "tensor"),
        P("dp", "tensor", "seq"),
        P("dp", "seq", "tensor"),
    )
    return jax.shard_map(
        local,
        mesh=mesh,
        in_specs=placed,
        out_specs=(
            P("dp", "seq", "tensor"),
            P("dp", "seq", "tensor"),
            P("dp", "seq", "tensor"),
            P("dp", "seq", "tensor"),
            P("tensor"),
        ),
        check_vma=False,
    )
```

```python
import functools
import math

import jax
import jax.numpy as jnp
from jax import lax
from jax.experimental import pallas as pl
from jax.experimental.pallas import tpu as pltpu
from jax.sharding import PartitionSpec as P

HEAD_SIZE = 128
D = 3584
LONGEST_WINDOW = 512
VMEM_LIMIT = 62 * 1024 * 1024
WRITE_LIMIT = 4 * 1024 * 1024

MESH = pl.DeviceIdType.MESH
f32 = jnp.float32
bf16 = jnp.bfloat16
precise = lax.Precision.HIGHEST
epsilon = 1e-06


def nn(left, right):
    return lax.dot_general(left, right, (((1,), (0,)), ((), ())), preferred_element_type=f32)


def nt(left, right):
    return lax.dot_general(left, right, (((1,), (1,)), ((), ())), preferred_element_type=f32)


def turned(block):
    return block.astype(f32).T


def kernel(
    sizes,
    q_hbm,
    k_hbm,
    v_hbm,
    window_ref,
    gain_hbm,
    level_hbm,
    lq_hbm,
    lk_hbm,
    decay_hbm,
    ct_hbm,
    out_ref,
    qg_ref,
    kg_ref,
    vg_ref,
    gg_ref,
    q_ref,
    k_ref,
    v_ref,
    gain_ref,
    level_ref,
    lq_ref,
    lk_ref,
    decay_ref,
    ct_ref,
    fetch_sems,
    pair_prev,
    probs,
    prob_grad_buf,
    heads_out,
    decayed,
    ct_turned,
    gain_cols,
    level_cols,
    ratio_cols,
    bounded_buf,
    spikes_buf,
    work,
    out_grads,
    logit_grads,
    weights_buf,
    part_one,
    part_two,
    square_slots,
    slope_slots,
    state_out,
    state_in,
    after_out,
    after_in,
    gain_slots,
    gain_sum_slots,
    pair_out,
    pair_in,
    pair_send,
    pair_recv,
    square_send,
    square_recv,
    state_send,
    state_recv,
    after_send,
    after_recv,
    slope_send,
    slope_recv,
    dp_send,
    dp_recv,
    seq_send,
    seq_recv,
    grad_send,
    grad_recv,
):
    n_seq, n_dp, n_tensor, previous, heads = sizes
    seq, dp, ten = lax.axis_index("seq"), lax.axis_index("dp"), lax.axis_index("tensor")
    size = HEAD_SIZE
    scaling = 1.0 / math.sqrt(HEAD_SIZE)
    cols = [slice(h * size, (h + 1) * size) for h in range(heads)]

    barrier = pltpu.get_barrier_semaphore()
    for axis, me, count in (("seq", seq, n_seq), ("dp", dp, n_dp), ("tensor", ten, n_tensor)):
        for step in range(1, count):
            pl.semaphore_signal(
                barrier,
                inc=1,
                device_id={axis: lax.rem(me + step, count)},
                device_id_type=MESH,
            )
    fetches = [
        pltpu.make_async_copy(source, target, fetch_sems.at[i])
        for i, (source, target) in enumerate(
            (
                (k_hbm, k_ref),
                (q_hbm, q_ref),
                (v_hbm, v_ref),
                (decay_hbm, decay_ref),
                (gain_hbm, gain_ref),
                (level_hbm, level_ref),
                (lk_hbm, lk_ref),
                (lq_hbm, lq_ref),
                (ct_hbm, ct_ref),
            )
        )
    ]
    for fetch in fetches:
        fetch.start()
    pl.semaphore_wait(barrier, n_seq + n_dp + n_tensor - 3)

    def remote(src, dst, send, recv, axis, target):
        return pltpu.make_async_remote_copy(
            src_ref=src,
            dst_ref=dst,
            send_sem=send,
            recv_sem=recv,
            device_id={axis: target},
            device_id_type=MESH,
        )

    def exchange(slots, send, recv, axis, me, count):
        def start():
            for step in range(1, count):
                remote(
                    slots.at[me],
                    slots.at[me],
                    send.at[step - 1],
                    recv.at[me],
                    axis,
                    lax.rem(me + step, count),
                ).start()

        def wait():
            for step in range(1, count):
                sender = lax.rem(me + count - step, count)
                copy = remote(
                    slots.at[me], slots.at[sender], send.at[step - 1], recv.at[sender], axis, sender
                )
                copy.wait_recv()

        def drain():
            for step in range(1, count):
                remote(
                    slots.at[me],
                    slots.at[me],
                    send.at[step - 1],
                    recv.at[me],
                    axis,
                    lax.rem(me + step, count),
                ).wait_send()

        return start, wait, drain

    def pair_copy(index, distance):
        source = (k_hbm, v_hbm)[index].at[0]
        return remote(
            source,
            pair_prev.at[index, distance - 1],
            pair_send.at[index, distance - 1],
            pair_recv.at[index, distance - 1],
            "seq",
            lax.rem(seq + distance, n_seq),
        )

    def grad_copy(index, distance):
        return remote(
            pair_out.at[index, distance - 1],
            pair_in.at[index, distance - 1],
            grad_send.at[index, distance - 1],
            grad_recv.at[index, distance - 1],
            "seq",
            lax.rem(seq + n_seq - distance, n_seq),
        )

    for distance in range(1, previous + 1):

        @pl.when(seq + distance < n_seq)
        def _():
            pair_copy(0, distance).start()
            pair_copy(1, distance).start()

        @pl.when(seq < distance)
        def _():
            for index in range(2):
                pair_prev[index, distance - 1] = jnp.zeros((size, size), bf16)

    row_index = lax.broadcasted_iota(jnp.int32, (size, size), 0)
    column_index = lax.broadcasted_iota(jnp.int32, (size, size), 1)
    causal = row_index <= column_index
    window = window_ref[0]
    for fetch in fetches[:3]:
        fetch.wait()
    keys = k_ref[0]
    values = v_ref[0]
    keys_turned = turned(keys).astype(bf16)
    values_turned = turned(values).astype(bf16)

    for h in range(heads):
        scores = nt(keys, q_ref[0, :, cols[h]]) * scaling
        probs[0, h] = jnp.where(causal, scores, -jnp.inf)

    def attend(blocks):
        squares = jnp.zeros((size, size), f32)
        block_keys = [pair_prev[0, d] for d in range(blocks)]
        block_values = [turned(pair_prev[1, d]).astype(bf16) for d in range(blocks)]
        masks = []
        for d in range(blocks):
            seen = (d + 1) * size + column_index - row_index < window
            masks.append(seen & (seq > d) if n_seq > 2 else seen)
        for h in range(heads):
            for d in range(blocks):
                score = nt(block_keys[d], q_ref[0, :, cols[h]]) * scaling
                probs[d + 1, h] = jnp.where(masks[d], score, -jnp.inf)
        for h in range(heads):
            scores = [probs[d, h] for d in range(blocks + 1)]
            top = functools.reduce(
                jnp.maximum, [jnp.max(score, axis=0, keepdims=True) for score in scores]
            )
            exponents = [jnp.exp(score - top) for score in scores]
            total = sum(jnp.sum(exponent, axis=0, keepdims=True) for exponent in exponents)
            share = 1.0 / total
            for d, exponent in enumerate(exponents):
                prob = exponent * share
                probs[d, h] = prob
                weights_buf[d, :, cols[h]] = prob.astype(bf16)
        for h in range(heads):
            result = None
            for d in range(blocks + 1):
                weights = weights_buf[d, :, cols[h]]
                part = nn(values_turned if d == 0 else block_values[d - 1], weights)
                result = part if result is None else result + part
            result = result.astype(bf16).astype(f32)
            heads_out[h] = result
            squares = squares + result * result
        part_one[...] = jnp.broadcast_to(jnp.sum(squares, axis=0, keepdims=True), (8, size))

    @pl.when(seq == 0)
    def _():
        attend(0)

    if previous:

        @pl.when(seq > 0)
        def _():
            for distance in range(1, previous + 1):

                @pl.when(seq >= distance)
                def _():
                    pair_copy(0, distance).wait_recv()
                    pair_copy(1, distance).wait_recv()

            attend(previous)

    square_slots[ten] = part_one[...]
    start, wait_squares, drain_squares = exchange(
        square_slots, square_send, square_recv, "tensor", ten, n_tensor
    )
    start()

    for fetch in fetches[3:]:
        fetch.wait()
    logs = decay_ref[:, 0, :]
    upper = jnp.where(causal, 1.0, 0.0)
    cumulative = jnp.dot(logs, upper, precision=precise, preferred_element_type=f32)
    whole = jnp.dot(
        logs, jnp.ones((size, size), f32), precision=precise, preferred_element_type=f32
    )
    tail = jnp.exp(jnp.minimum(whole - cumulative, 0.0))
    grown = jnp.exp(cumulative)
    block_decay = jnp.exp(whole)
    for h in range(heads):
        level_rows = jnp.broadcast_to(level_ref[h : h + 1, :].astype(f32), (size, size))
        gain_rows = jnp.broadcast_to(gain_ref[h : h + 1, :], (size, size))
        level_cols[h] = level_rows.T
        gain_cols[h] = gain_rows.T
        ratio_cols[h] = gain_cols[h] / level_cols[h]
        ct_turned[h] = turned(ct_ref[0, :, cols[h]])
        along = jnp.broadcast_to(cumulative[h : h + 1, :], (size, size))
        gaps = jnp.where(causal, along - along.T, -jnp.inf)
        product = nt(lk_ref[0, :, cols[h]], lq_ref[0, :, cols[h]])
        decayed[h] = (jnp.exp(gaps) * product).astype(bf16)

    wait_squares()
    square_sum = sum(square_slots[i] for i in range(n_tensor))[:1]
    inverse = lax.rsqrt(square_sum / D + epsilon)

    half = (heads + 1) // 2
    groups = [range(half), range(half, heads)]

    def state_copy(g):
        part = pl.ds(groups[g][0], len(groups[g]))
        return remote(
            state_out.at[part],
            state_in.at[part],
            state_send.at[g],
            state_recv.at[g],
            "seq",
            lax.rem(seq + 1, n_seq),
        )

    def after_copy(g):
        part = pl.ds(groups[g][0], len(groups[g]))
        return remote(
            after_out.at[part],
            after_in.at[part],
            after_send.at[g],
            after_recv.at[g],
            "seq",
            lax.rem(seq + n_seq - 1, n_seq),
        )

    for g, group in enumerate(groups):
        for h in group:
            normed = heads_out[h] * inverse
            heads_out[h] = normed
            bounded = jnp.tanh(normed * ratio_cols[h])
            bounded_buf[h] = bounded
            spikes = (level_cols[h] * bounded).astype(bf16)
            spikes_buf[h] = spikes
            fading = (spikes.astype(f32) * tail[h : h + 1]).astype(bf16)
            state_out[h] = nn(fading, lk_ref[0, :, cols[h]]).astype(state_out.dtype)
        if n_seq > 1:

            @pl.when(seq == 0)
            def _():
                state_copy(g).start()

    for h in range(heads):
        work[h] = nn(spikes_buf[h], decayed[h])

    if n_seq > 1:

        @pl.when(seq > 0)
        def _():
            for g, group in enumerate(groups):
                state_copy(g).wait_recv()
                if n_seq > 2:
                    for h in group:
                        state_out[h] = (
                            block_decay[h : h + 1] * state_in[h].astype(f32)
                            + state_out[h].astype(f32)
                        ).astype(state_out.dtype)

                    @pl.when(seq < n_seq - 1)
                    def _():
                        state_copy(g).start()

                for h in group:
                    carried = nt(state_in[h].astype(bf16), lq_ref[0, :, cols[h]])
                    work[h] = work[h] + grown[h : h + 1] * carried

    for g, group in enumerate(groups):
        for h in group:
            membrane = work[h]
            mean = jnp.sum(membrane * membrane, axis=0, keepdims=True) / size
            scale = lax.rsqrt(mean + epsilon)
            unit = membrane * scale
            incoming = ct_turned[h]
            inner = jnp.sum(incoming * unit, axis=0, keepdims=True) / size
            grad = scale * (incoming - unit * inner)
            ct_turned[h] = unit
            spikes_buf[h] = grad.astype(bf16)
            after_out[h] = nn((grad * grown[h : h + 1]).astype(bf16), lq_ref[0, :, cols[h]]).astype(
                after_out.dtype
            )
        if n_seq > 1:

            @pl.when(seq == n_seq - 1)
            def _():
                after_copy(g).start()

    for h in range(heads):
        work[h] = nt(spikes_buf[h], decayed[h])

    if n_seq > 1:

        @pl.when(seq < n_seq - 1)
        def _():
            for g, group in enumerate(groups):
                after_copy(g).wait_recv()
                if n_seq > 2:
                    for h in group:
                        after_out[h] = (
                            block_decay[h : h + 1] * after_in[h].astype(f32)
                            + after_out[h].astype(f32)
                        ).astype(after_out.dtype)

                    @pl.when(seq > 0)
                    def _():
                        after_copy(g).start()

                for h in group:
                    later = nt(after_in[h].astype(bf16), lk_ref[0, :, cols[h]])
                    work[h] = work[h] + tail[h : h + 1] * later

    slope_part = jnp.zeros((size, size), f32)
    for h in range(heads):
        bounded = bounded_buf[h]
        level_grad = work[h] * (1.0 - bounded * bounded)
        with_normed = level_grad * heads_out[h]
        work[h] = level_grad
        bounded_buf[h] = with_normed
        slope_part = slope_part + with_normed * gain_cols[h]
    part_two[...] = jnp.broadcast_to(jnp.sum(slope_part, axis=0, keepdims=True), (8, size))
    slope_slots[ten] = part_two[...]
    start, wait_slopes, drain_slopes = exchange(
        slope_slots, slope_send, slope_recv, "tensor", ten, n_tensor
    )
    start()

    rows = [jnp.sum(bounded_buf[h].T, axis=0, keepdims=True) for h in range(heads)]
    rows.append(jnp.zeros((8 - heads, size), f32))
    gain_slots[dp] = jnp.concatenate(rows, axis=0)
    start, wait_dp, drain_dp = exchange(gain_slots, dp_send, dp_recv, "dp", dp, n_dp)
    start()

    for h in range(heads):
        out_ref[0, :, cols[h]] = ct_turned[h].T.astype(bf16)

    wait_slopes()
    slope = sum(slope_slots[i] for i in range(n_tensor))[:1] / D
    for h in range(heads):
        normed_grad = work[h] * gain_cols[h]
        out_grads[:, cols[h]] = (inverse * (normed_grad - heads_out[h] * slope)).astype(bf16)

    def back(blocks):
        block_values = [values] + [pair_prev[1, d] for d in range(blocks)]
        for h in range(heads):
            for d, block in enumerate(block_values):
                prob_grad_buf[d, h] = nn(block, out_grads[:, cols[h]])
        for h in range(heads):
            prob_grads = [prob_grad_buf[d, h] for d in range(blocks + 1)]
            delta = sum(
                jnp.sum(probs[d, h] * prob_grad, axis=0, keepdims=True)
                for d, prob_grad in enumerate(prob_grads)
            )
            for d, prob_grad in enumerate(prob_grads):
                logit_grad = probs[d, h] * (prob_grad - delta) * scaling
                logit_grads[d, :, cols[h]] = logit_grad.astype(bf16)

    def key_sum(d):
        return sum(nn(logit_grads[d, :, cols[h]], q_ref[0, :, cols[h]]) for h in range(heads))

    def value_sum(d):
        return nt(weights_buf[d], out_grads[...])

    @pl.when(seq == 0)
    def _():
        back(0)

    if previous:

        @pl.when(seq > 0)
        def _():
            for distance in range(1, previous + 1):
                pair_out[1, distance - 1] = value_sum(distance)

                @pl.when(seq >= distance)
                def _():
                    grad_copy(1, distance).start()

            back(previous)
            for distance in range(1, previous + 1):
                pair_out[0, distance - 1] = key_sum(distance)

                @pl.when(seq >= distance)
                def _():
                    grad_copy(0, distance).start()

    wait_dp()
    gain_sum_slots[seq] = sum(gain_slots[i] for i in range(n_dp))
    start, wait_seq, drain_seq = exchange(gain_sum_slots, seq_send, seq_recv, "seq", seq, n_seq)
    start()

    @pl.when(seq == 0)
    def _():
        for h in range(heads):
            query_grad = nn(keys_turned, logit_grads[0, :, cols[h]])
            qg_ref[0, :, cols[h]] = query_grad.T.astype(bf16)

    if previous:

        @pl.when(seq > 0)
        def _():
            earlier = [turned(pair_prev[0, d]).astype(bf16) for d in range(previous)]
            for h in range(heads):
                query_grad = nn(keys_turned, logit_grads[0, :, cols[h]])
                for d in range(previous):
                    query_grad = query_grad + nn(earlier[d], logit_grads[d + 1, :, cols[h]])
                qg_ref[0, :, cols[h]] = query_grad.T.astype(bf16)

    pair_out[0, previous] = key_sum(0)
    pair_out[1, previous] = value_sum(0)
    wait_seq()
    gg_ref[...] = sum(gain_sum_slots[i] for i in range(n_seq))[:heads]

    for distance in range(1, previous + 1):

        @pl.when(seq + distance < n_seq)
        def _():
            for index in range(2):
                grad_copy(index, distance).wait_recv()
                pair_out[index, previous] = (
                    pair_out[index, previous] + pair_in[index, distance - 1]
                )

    kg_ref[0] = pair_out[0, previous].astype(bf16)
    vg_ref[0] = pair_out[1, previous].astype(bf16)

    for distance in range(1, previous + 1):

        @pl.when(seq + distance < n_seq)
        def _():
            pair_copy(0, distance).wait_send()
            pair_copy(1, distance).wait_send()

        @pl.when(seq >= distance)
        def _():
            grad_copy(0, distance).wait_send()
            grad_copy(1, distance).wait_send()

    if n_seq > 1:

        @pl.when(seq < n_seq - 1)
        def _():
            for g in range(2):
                state_copy(g).wait_send()

        @pl.when(seq > 0)
        def _():
            for g in range(2):
                after_copy(g).wait_send()

    drain_squares()
    drain_slopes()
    drain_dp()
    drain_seq()


def write_out(*refs):
    sources, targets, sems = refs[:5], refs[5:10], refs[10]
    writes = [pltpu.make_async_copy(sources[i], targets[i], sems.at[i]) for i in range(5)]
    for write in writes:
        write.start()
    for write in writes:
        write.wait()


def local(
    attention_queries,
    attention_keys,
    attention_values,
    key_window_length,
    norm_gain,
    spike_levels,
    lin_queries,
    lin_keys,
    decay_logs,
    cotangent,
):
    n_seq, n_dp, n_tensor = (lax.axis_size(axis) for axis in ("seq", "dp", "tensor"))
    rows = attention_queries.shape[1]
    heads = attention_queries.shape[2] // HEAD_SIZE
    previous = min((LONGEST_WINDOW + rows - 1) // rows, n_seq - 1)
    slots = max(previous, 1)
    state_type = bf16 if n_seq == 2 else f32
    size = HEAD_SIZE
    hbm = pl.BlockSpec(memory_space=pltpu.HBM)
    vmem = pl.BlockSpec(memory_space=pltpu.VMEM)
    smem = pl.BlockSpec(memory_space=pltpu.SMEM)
    tiles = (heads, size, size)
    dma = pltpu.SemaphoreType.DMA
    outputs = (
        jax.ShapeDtypeStruct(attention_queries.shape, bf16),
        jax.ShapeDtypeStruct(attention_queries.shape, bf16),
        jax.ShapeDtypeStruct(attention_keys.shape, bf16),
        jax.ShapeDtypeStruct(attention_keys.shape, bf16),
        jax.ShapeDtypeStruct((heads, size), f32),
    )
    wide = pltpu.VMEM(attention_queries.shape, bf16)
    narrow = pltpu.VMEM(attention_keys.shape, bf16)
    scratch = [
        wide,
        narrow,
        narrow,
        pltpu.VMEM((heads, size), f32),
        pltpu.VMEM((heads, size), jnp.int32),
        wide,
        wide,
        pltpu.VMEM((heads, 1, size), f32),
        wide,
        dma((9,)),
        pltpu.VMEM((2, slots, size, size), bf16),
        pltpu.VMEM((previous + 1,) + tiles, f32),
        pltpu.VMEM((previous + 1,) + tiles, f32),
        pltpu.VMEM(tiles, f32),
        pltpu.VMEM(tiles, bf16),
        pltpu.VMEM(tiles, f32),
        pltpu.VMEM(tiles, f32),
        pltpu.VMEM(tiles, f32),
        pltpu.VMEM(tiles, f32),
        pltpu.VMEM(tiles, f32),
        pltpu.VMEM(tiles, bf16),
        pltpu.VMEM(tiles, f32),
        pltpu.VMEM((size, heads * size), bf16),
        pltpu.VMEM((previous + 1, size, heads * size), bf16),
        pltpu.VMEM((previous + 1, size, heads * size), bf16),
        pltpu.VMEM((8, size), f32),
        pltpu.VMEM((8, size), f32),
        pltpu.VMEM((n_tensor, 8, size), f32),
        pltpu.VMEM((n_tensor, 8, size), f32),
        pltpu.VMEM(tiles, state_type),
        pltpu.VMEM(tiles, state_type),
        pltpu.VMEM(tiles, state_type),
        pltpu.VMEM(tiles, state_type),
        pltpu.VMEM((n_dp, 8, size), f32),
        pltpu.VMEM((n_seq, 8, size), f32),
        pltpu.VMEM((2, previous + 1, size, size), f32),
        pltpu.VMEM((2, slots, size, size), f32),
        dma((2, slots)),
        dma((2, slots)),
        dma((n_tensor,)),
        dma((n_tensor,)),
        dma((2,)),
        dma((2,)),
        dma((2,)),
        dma((2,)),
        dma((n_tensor,)),
        dma((n_tensor,)),
        dma((n_dp,)),
        dma((n_dp,)),
        dma((n_seq,)),
        dma((n_seq,)),
        dma((2, slots)),
        dma((2, slots)),
    ]
    results = pl.pallas_call(
        functools.partial(kernel, (n_seq, n_dp, n_tensor, previous, heads)),
        out_shape=tuple(pltpu.VMEM(out.shape, out.dtype) for out in outputs),
        in_specs=[hbm, hbm, hbm, smem] + [hbm] * 6,
        out_specs=(vmem,) * 5,
        scratch_shapes=scratch,
        compiler_params=pltpu.CompilerParams(
            collective_id=0, has_side_effects=True, vmem_limit_bytes=VMEM_LIMIT
        ),
        name="layer_pair",
    )(
        attention_queries,
        attention_keys,
        attention_values,
        key_window_length,
        norm_gain.reshape(heads, size),
        spike_levels.reshape(heads, size),
        lin_queries,
        lin_keys,
        decay_logs.reshape(heads, 1, rows),
        cotangent,
    )
    layer_output, query_grads, key_gradient, value_gradient, gain_grads = pl.pallas_call(
        write_out,
        out_shape=outputs,
        in_specs=[vmem] * 5,
        out_specs=(hbm,) * 5,
        scratch_shapes=[dma((5,))],
        compiler_params=pltpu.CompilerParams(vmem_limit_bytes=WRITE_LIMIT),
        name="write_out",
    )(*results)
    return (layer_output, query_grads, key_gradient, value_gradient, gain_grads.reshape(-1))


def solution(mesh):
    placed = (
        P("dp", "seq", "tensor"),
        P("dp", "seq", "tensor"),
        P("dp", "seq", "tensor"),
        P("tensor"),
        P("tensor"),
        P("tensor"),
        P("dp", "seq", "tensor"),
        P("dp", "seq", "tensor"),
        P("dp", "tensor", "seq"),
        P("dp", "seq", "tensor"),
    )
    return jax.shard_map(
        local,
        mesh=mesh,
        in_specs=placed,
        out_specs=(
            P("dp", "seq", "tensor"),
            P("dp", "seq", "tensor"),
            P("dp", "seq", "tensor"),
            P("dp", "seq", "tensor"),
            P("tensor"),
        ),
        check_vma=False,
    )
```
